512 devices in a mesh: seg: 128 (over y_hi, z, x), tp: 4 (over y_lo, core).
Axes of the slice: x: 4, y: 8 (y_hi: 4, y_lo: 2; y = y_hi * 2 + y_lo), z: 8, core: 2. Of those that a mesh axis runs over, the one named last changes fastest.
Arguments:
- inputs: bfloat16 [16384, 2048], P('seg', 'tp'), may hold values from -40 to 40
- cotangent: bfloat16 [16384, 2048], P('seg', 'tp'), may hold values from -6 to 6
- w_query: bfloat16 [2, 2048, 2048], P(None, 'seg', 'tp'), may hold values from -1 to 1
- w_key: bfloat16 [2, 2048, 2048], P(None, 'seg', 'tp'), may hold values from -1 to 1
- w_value: bfloat16 [2, 2048, 2048], P(None, 'seg', 'tp'), may hold values from -0.25 to 0.25
- boundary: int32 [128], replicated, may hold values from 0 to 128, as said below
Outputs:
- outputs: bfloat16 [16384, 2048], P('seg', 'tp')
- input_grad: float32 [16384, 2048], P('seg', 'tp')
The draws below stay inside these ranges and needn't reach their ends.
Inputs may be any that keep to these rules, and one draw needn't show every extreme that they name: `boundary`: the first segment's value is 0, the second's and the last segment's are 128; the value 128 means that no utterance begins in the segment.
All inputs are finite; a program needn't handle non-finite values.
Results may differ from the reference program's by a relative error of at most 0.035.
Values may be sent and summed in bfloat16 or wider, within the bound.
A program may use at most 64 MiB of HBM per device.

```python
import math
import jax
import jax.numpy as jnp
from jax import lax

D = 2048
HEADS = 16
HEAD = 128
LAYERS = 2
ROWS = 128
SEGS = 128
ROWS_ALL = 16384


def draw_w_query(key, part):
    key = jax.random.fold_in(key, 3)
    private = jax.random.normal(key, (LAYERS, D, D), jnp.float32) * D ** (-0.5)
    result = private
    return jnp.clip(result, -1.0, 1.0).astype(jnp.bfloat16)


def draw_w_key(key, part):
    key = jax.random.fold_in(key, 5)
    private = jax.random.normal(key, (LAYERS, D, D), jnp.float32) * D ** (-0.5)
    result = private
    return jnp.clip(result, -1.0, 1.0).astype(jnp.bfloat16)


def draw_inputs(key, part):
    key = jax.random.fold_in(key, 11)
    key_base = jax.random.fold_in(key, 0)
    base = jax.random.normal(key_base, (ROWS_ALL, D), jnp.float32)
    result = jnp.clip(base, -6.0, 6.0)
    return result.astype(jnp.bfloat16)


def draw_boundary(key, part):
    key = jax.random.fold_in(key, 7)
    values = jax.random.randint(key, (SEGS,), 0, ROWS + 1, dtype=jnp.int32)
    values = values.at[0].set(0)
    values = values.at[1].set(ROWS)
    values = values.at[SEGS - 1].set(ROWS)
    return values


def block_levels(own_key, shape, cuts, low, high):
    factor_of, own = 1.0, jax.random.fold_in(own_key, 6)
    for axis_at, parts in cuts:
        steps = jnp.exp(jax.random.uniform(jax.random.fold_in(own, axis_at), (parts,), jnp.float32, low / len(cuts), high / len(cuts)))
        factor_of = factor_of * jnp.repeat(steps, shape[axis_at] // parts).reshape([-1 if axis == axis_at else 1 for axis in range(len(shape))])
    return factor_of


def noise(key, shape, deviation, reach, cuts=(), kind=jnp.bfloat16):
    gain = block_levels(key, shape, cuts, -0.22, 0.18) if cuts else 1.0
    drawn = jax.random.normal(key, shape, jnp.float32) * deviation * gain
    return jnp.minimum(jnp.maximum(drawn, -reach), reach).astype(kind)


def setup_inputs(seed: int = 0) -> dict:
    key_of = jax.random.split(jax.random.key(seed), 7)
    inputs = draw_inputs(jax.random.fold_in(key_of[6], 71), 0)
    cotangent = noise(key_of[1], (ROWS_ALL, D), 1.0, 6.0, ((0, 128), (1, 4)))
    w_query = draw_w_query(jax.random.fold_in(key_of[6], 71), 0)
    w_key = draw_w_key(jax.random.fold_in(key_of[6], 71), 0)
    w_value = noise(key_of[4], (LAYERS, D, D), (D // 4) ** -0.5, 0.25, ((1, 128), (2, 4)))
    boundary = draw_boundary(jax.random.fold_in(key_of[6], 71), 0)
    return dict(inputs=inputs, cotangent=cotangent, w_query=w_query, w_key=w_key, w_value=w_value, boundary=boundary)


def visibility(boundary):
    positions = jnp.arange(ROWS, dtype=jnp.int32)
    query_pos = positions[None, :, None]
    key_pos = positions[None, None, :]
    bound_now = boundary[:, None, None]
    bound_prev = jnp.concatenate([jnp.zeros((1,), jnp.int32), boundary[:-1]])
    first_live = jnp.where(bound_prev == ROWS, 0, bound_prev)[:, None, None]
    seg_ids = jnp.arange(SEGS, dtype=jnp.int32)[:, None, None]
    from_memory = (query_pos < bound_now) & (key_pos >= first_live) & (seg_ids > 0)
    from_segment = (key_pos <= query_pos) & jnp.logical_not((key_pos < bound_now) & (query_pos >= bound_now))
    return jnp.concatenate([from_memory, from_segment], axis=2)[:, None]

def split_heads(matrix):
    return matrix.reshape(SEGS, ROWS, HEADS, HEAD)

def with_memory(heads_array):
    earlier = jnp.concatenate([jnp.zeros_like(heads_array[:1]), heads_array[:-1]], axis=0)
    return jnp.concatenate([earlier, heads_array], axis=1)

def forward_layer(states, query_weight, key_weight, value_weight, visible):
    score_scale = 1.0 / math.sqrt(HEAD)
    queries = jnp.dot(states, query_weight, preferred_element_type=jnp.float32).astype(jnp.bfloat16)
    key_rows = jnp.dot(states, key_weight, preferred_element_type=jnp.float32).astype(jnp.bfloat16)
    value_rows = jnp.dot(states, value_weight, preferred_element_type=jnp.float32).astype(jnp.bfloat16)
    query_heads = split_heads(queries)
    all_keys = with_memory(split_heads(key_rows))
    all_values = with_memory(split_heads(value_rows))
    scores = jnp.einsum('srhe,sjhe->shrj', query_heads.astype(jnp.float32), all_keys.astype(jnp.float32)) * score_scale
    scores = jnp.where(visible, scores, -1e+30)
    maxima = lax.optimization_barrier(jnp.max(scores, axis=-1, keepdims=True))
    raised = jnp.exp(scores - maxima)
    attn_weights = (raised / lax.optimization_barrier(jnp.sum(raised, axis=-1, keepdims=True))).astype(jnp.bfloat16)
    attended = jnp.einsum('shrj,sjhe->srhe', attn_weights.astype(jnp.float32), all_values.astype(jnp.float32))
    following = (states.astype(jnp.float32) + attended.reshape(ROWS_ALL, D)).astype(jnp.bfloat16)
    return (following, (query_heads, all_keys, all_values, attn_weights))

def settle(grad_both):
    later = jnp.concatenate([grad_both[1:, :ROWS], jnp.zeros_like(grad_both[:1, :ROWS])], axis=0)
    return (grad_both[:, ROWS:] + later).astype(jnp.bfloat16).reshape(ROWS_ALL, D)

def backward_layer(grad, saved, query_weight, key_weight, value_weight):
    score_scale = 1.0 / math.sqrt(HEAD)
    query_heads, all_keys, all_values, attn_weights = saved
    grad_out = grad.astype(jnp.bfloat16).reshape(SEGS, ROWS, HEADS, HEAD).astype(jnp.float32)
    grad_probs = jnp.einsum('srhe,sjhe->shrj', grad_out, all_values.astype(jnp.float32))
    weights_float = attn_weights.astype(jnp.float32)
    row_dots = lax.optimization_barrier(jnp.sum(weights_float * grad_probs, axis=-1, keepdims=True))
    grad_scores = (weights_float * (grad_probs - row_dots) * score_scale).astype(jnp.bfloat16).astype(jnp.float32)
    grad_query = jnp.einsum('shrj,sjhe->srhe', grad_scores, all_keys.astype(jnp.float32))
    grad_keys = jnp.einsum('shrj,srhe->sjhe', grad_scores, query_heads.astype(jnp.float32))
    grad_values = jnp.einsum('shrj,srhe->sjhe', weights_float, grad_out)
    query_part = grad_query.astype(jnp.bfloat16).reshape(ROWS_ALL, D)
    partial_value = jnp.dot(query_part, query_weight.T, preferred_element_type=jnp.float32)
    partial_value = partial_value + jnp.dot(settle(grad_keys), key_weight.T, preferred_element_type=jnp.float32)
    partial_value = partial_value + jnp.dot(settle(grad_values), value_weight.T, preferred_element_type=jnp.float32)
    return grad + partial_value

def reference(inputs, cotangent, w_query, w_key, w_value, boundary):
    visible = visibility(boundary)
    states = inputs
    saved_all = []
    for layer_id in range(LAYERS):
        states, saved = forward_layer(states, w_query[layer_id], w_key[layer_id], w_value[layer_id], visible)
        saved_all.append(saved)
    grad = cotangent.astype(jnp.float32)
    for layer_id in reversed(range(LAYERS)):
        grad = backward_layer(grad, saved_all[layer_id], w_query[layer_id], w_key[layer_id], w_value[layer_id])
    return (states, grad)
```

```python
import math

import jax
import jax.numpy as jnp
from jax import lax
from jax.experimental import pallas as pl
from jax.experimental.pallas import tpu as pltpu
from jax.sharding import PartitionSpec as P

MESH = pl.DeviceIdType.MESH
HEAD = 128
LAYERS = 2
ROWS = 128
D = 2048
GROUP_ROWS = 2 * ROWS
BLK = 2 * HEAD
SCALE = 1.0 / math.sqrt(HEAD)
N_SEND = 176
N_RECV = 176
BF = jnp.bfloat16
F32 = jnp.float32


def nt(a, b):
    return lax.dot_general(a, b, (((1,), (1,)), ((), ())), preferred_element_type=F32)


def nn(a, b):
    return lax.dot_general(a, b, (((1,), (0,)), ((), ())), preferred_element_type=F32)


def tn(a, b):
    return lax.dot_general(a, b, (((0,), (0,)), ((), ())), preferred_element_type=F32)


def kernel(
    x_in, cot_in, wq, wk, wv, bound,
    out_ref, grad_ref,
    stage, w, x0, x1, cotg, kv, q, probs, dkv, halo_send, halo_recv, dqkv,
    swap_send, swap_recv, own, rs_send, rs1_recv, rs0_recv, x2, outbuf, g1,
    ssem, rsem,
):
    seg = lax.axis_index("seg")
    tp = lax.axis_index("tp")
    x = lax.rem(seg, 4)
    z = lax.rem(lax.div(seg, 4), 8)
    yh = lax.div(seg, 32)
    yl = lax.div(tp, 2)
    c = lax.rem(tp, 2)
    y = yh * 2 + yl
    other = 1 - c
    xh = lax.div(x, 2)
    xl = lax.rem(x, 2)

    def dev(dx, dy, dz, dc):
        return (lax.div(dy, 2) * 32 + dz * 4 + dx, lax.rem(dy, 2) * 2 + dc)

    def wrap(value, n):
        return lax.rem(value + n, n)

    me_y = y
    pair_y = yh * 2 + (1 - yl)
    group = yh * 16 + z * 2 + yl
    after = wrap(group + 1, 64)
    before = wrap(group - 1, 64)

    def group_dev(g):
        gy = lax.div(g, 16) * 2 + lax.rem(g, 2)
        return dev(x, gy, lax.rem(lax.div(g, 2), 8), c)

    partner = dev(x, y, z, other)
    peers = [dev(wrap(x + k, 4), y, z, c) for k in (1, 2, 3)]

    counts = {"s": 0, "r": 0}
    pending = []

    def take(kind, n=1):
        first = counts[kind]
        counts[kind] += n
        return first

    def send(src, dst, recv, target, cond=None):
        copy = pltpu.make_async_remote_copy(
            src_ref=src, dst_ref=dst, send_sem=ssem.at[take("s")], recv_sem=rsem.at[recv],
            device_id=target, device_id_type=MESH,
        )
        if cond is None:
            copy.start()
        else:
            pl.when(cond)(copy.start)
        pending.append((copy, cond))

    def arrive(dst, recv, cond=None):
        copy = pltpu.make_async_remote_copy(
            src_ref=dst, dst_ref=dst, send_sem=ssem.at[0], recv_sem=rsem.at[recv],
            device_id=partner, device_id_type=MESH,
        )
        if cond is None:
            copy.wait_recv()
        else:
            pl.when(cond)(copy.wait_recv)

    for layer in range(LAYERS):
        for j in range(2):
            for t, ref in enumerate((wq, wk, wv)):
                stage[j, layer, :, t * BLK:(t + 1) * BLK] = ref[layer, :, j * BLK:(j + 1) * BLK]

    barrier = pltpu.get_barrier_semaphore()
    known = list(peers) + [partner, group_dev(after), group_dev(before)]
    known += [dev(wrap(x + k, 4), pair_y, z, c) for k in (1, 2, 3)]
    known += [dev(x, y, wrap(z + k, 8), c) for k in range(1, 8)]
    known += [dev(x, wrap(y + k, 8), z, c) for k in range(1, 8)]
    for device in known:
        pl.semaphore_signal(barrier, inc=1, device_id=device, device_id_type=MESH)
    pl.semaphore_wait(barrier, len(known))

    same = xh == yl
    home = [same & (xl == j) for j in range(2)]
    away = [jnp.logical_not(h) for h in home]
    dest_y = yh * 2 + xh
    own_col = pl.multiple_of(xh * 1024 + c * 512 + xl * BLK, BLK)

    a2a_w = [take("r", 2) for _ in range(LAYERS)]
    a2a_c = take("r", 2)

    def spread_weights(layer):
        for j in range(2):
            dst = w.at[layer, yh, z, xh, xl]
            send(stage.at[j, layer], dst, a2a_w[layer] + xl, dev(2 * yl + j, dest_y, z, c), away[j])

            @pl.when(home[j])
            def _():
                w[layer, yh, z, xh, xl] = stage[j, layer]

    def spread_weights_wait(layer):
        for k in range(2):
            arrive(w.at[layer, yh, z, yl, k], a2a_w[layer] + k, away[k])

    spread_weights(0)
    spread_weights(1)

    x0_x = [[take("r") for _ in range(2)] for _ in range(2)]
    x0_c = [[take("r") for _ in range(2)] for _ in range(2)]
    my_rows = pl.multiple_of(xl * ROWS, ROWS)
    my_cols = pl.multiple_of(tp * 512, 512)

    @pl.when(same)
    def _():
        x0[pl.ds(my_rows, ROWS), pl.ds(my_cols, 512)] = x_in[...]

    send(
        x_in, x0.at[pl.ds(my_rows, ROWS), pl.ds(my_cols, 512)], x0_x[0][0] + xl * 2 + yl,
        dev(x, pair_y, z, c), jnp.logical_not(same),
    )

    def x0_piece(j, half, core):
        return x0.at[pl.ds(j * ROWS, ROWS), pl.ds(pl.multiple_of(half * 1024 + core * 512, 512), 512)]

    def x0_step(j, half, local):
        piece = x0_piece(j, half, c)
        here = home[j] & (yl == half)
        if not local:
            arrive(piece, x0_x[j][half], jnp.logical_not(here))
        for target in peers:
            cond = here if local else home[j] & (yl != half)
            send(piece, piece, x0_x[j][half], target, cond)

    def x0_swap(j, half):
        piece = x0_piece(j, half, c)
        send(piece, piece, x0_c[j][half], partner)

    for j in range(2):
        for half in range(2):
            x0_step(j, half, True)

    for j in range(2):
        dst = cotg.at[pl.ds(my_rows, ROWS)]
        src = cot_in.at[:, pl.ds(j * BLK, BLK)]
        send(src, dst, a2a_c + xl, dev(2 * yl + j, dest_y, z, c), away[j])

        @pl.when(home[j])
        def _():
            cotg[pl.ds(my_rows, ROWS)] = cot_in[:, j * BLK:(j + 1) * BLK]

    one = [[take("r", 7) for _ in range(2)] for _ in range(LAYERS)]
    two = {
        (layer, kind, right, s, d): take("r")
        for layer in range(LAYERS) for d in range(1, 5) for kind in range(2) for right in range(2) for s in range(2)
        if d <= (4 if right == s else 3)
    }

    def phase_one(layer):
        for k in range(1, 8):
            a = w.at[layer, yh, z, yl, 0]
            send(a, a, one[layer][0] + k - 1, dev(x, y, wrap(z + k, 8), c))
            b = w.at[layer, yh, z, yl, 1]
            send(b, b, one[layer][1] + k - 1, dev(x, wrap(y + k, 8), z, c))

    def phase_one_wait(layer):
        for k in range(1, 8):
            arrive(w.at[layer, yh, wrap(z - k, 8), yl, 0], one[layer][0] + k - 1)
            ys = wrap(y - k, 8)
            arrive(w.at[layer, lax.div(ys, 2), z, lax.rem(ys, 2), 1], one[layer][1] + k - 1)

    def chunk(layer, kind, right, s, d):
        if kind == 0:
            ys = wrap(y - d if right else y + d, 8)
            return w.at[layer, lax.div(ys, 2), pl.ds(4 * s, 4), lax.rem(ys, 2), 0]
        zs = wrap(z - d if right else z + d, 8)
        return w.at[layer, pl.ds(2 * s, 2), zs, :, 1]

    def forward(layer, kind, right, s, d):
        step = 1 if right else -1
        target = dev(x, wrap(y + step, 8), z, c) if kind == 0 else dev(x, y, wrap(z + step, 8), c)
        piece = chunk(layer, kind, right, s, d)
        send(piece, piece, two[layer, kind, right, s, d + 1], target)

    def phase_two(layer, d):
        for s in range(2):
            for kind in range(2):
                for right in range(2):
                    most = 4 if right == s else 3
                    if d > most:
                        continue
                    if d > 0:
                        arrive(chunk(layer, kind, right, s, d), two[layer, kind, right, s, d])
                    if d < most:
                        forward(layer, kind, right, s, d)

    spread_weights_wait(0)
    phase_one(0)
    spread_weights_wait(1)
    phase_one_wait(0)
    phase_two(0, 0)
    phase_one(1)
    for j in range(2):
        for half in range(2):
            x0_step(j, half, False)
    phase_two(0, 1)
    for j in range(2):
        for half in range(2):
            x0_swap(j, half)
    phase_two(0, 2)
    phase_two(0, 3)
    phase_one_wait(1)
    phase_two(1, 0)
    phase_two(0, 4)
    for j in range(2):
        for half in range(2):
            arrive(x0_piece(j, half, other), x0_c[j][half])

    pos_q = lax.broadcasted_iota(jnp.int32, (ROWS, GROUP_ROWS), 0)
    pos_k = lax.broadcasted_iota(jnp.int32, (ROWS, GROUP_ROWS), 1)

    def mask(j):
        s = 2 * group + j
        now = bound[s]
        prev = bound[jnp.maximum(s - 1, 0)]
        first = jnp.where(prev == ROWS, 0, prev)
        first = jnp.where(s > 0, first, ROWS)
        pos_m = pos_k - ROWS
        memory = (pos_k < ROWS) & (pos_q < now) & (pos_k >= first)
        segment = (pos_m >= 0) & (pos_m <= pos_q) & ((pos_m >= now) | (pos_q < now))
        return memory | segment

    halo_f = [take("r") for _ in range(LAYERS)]
    halo_b = [take("r") for _ in range(LAYERS)]

    def project(layer, states):
        total = None
        for part in range(4):
            weight = w[layer, part].reshape(512, 3 * BLK)
            term = nn(states[:, part * 512:(part + 1) * 512], weight)
            total = term if total is None else total + term
        total = total.astype(BF)
        q[layer] = total[:, :BLK]
        kv[layer, ROWS:, :] = total[:, BLK:]
        tail = kv.at[layer, pl.ds(2 * ROWS, ROWS)]
        send(tail, kv.at[layer, pl.ds(0, ROWS)], halo_f[layer], group_dev(after))

    def attend(layer, j):
        visible = mask(j)
        results = []
        for h in range(2):
            cols = slice(h * HEAD, (h + 1) * HEAD)
            vcols = slice(BLK + h * HEAD, BLK + (h + 1) * HEAD)
            queries = q[layer, j * ROWS:(j + 1) * ROWS, cols]
            keys = kv[layer, j * ROWS:(j + 2) * ROWS, cols]
            values = kv[layer, j * ROWS:(j + 2) * ROWS, vcols]
            scores = jnp.where(visible, nt(queries, keys) * SCALE, -1e30)
            raised = jnp.exp(scores - jnp.max(scores, axis=-1, keepdims=True))
            share = (raised / jnp.sum(raised, axis=-1, keepdims=True)).astype(BF)
            probs[layer, j, h] = share
            results.append(nn(share, values))
        return jnp.concatenate(results, axis=1)

    def x1_piece(j, xs, core):
        col = lax.div(xs, 2) * 1024 + core * 512 + lax.rem(xs, 2) * BLK
        return x1.at[pl.ds(j * ROWS, ROWS), pl.ds(pl.multiple_of(col, BLK), BLK)]

    x1_x = [take("r", 3) for _ in range(2)]
    x1_c = [take("r", 4) for _ in range(2)]

    def step_states(j):
        before_states = x0[j * ROWS:(j + 1) * ROWS, pl.ds(own_col, BLK)]
        x1[j * ROWS:(j + 1) * ROWS, pl.ds(own_col, BLK)] = (
            before_states.astype(F32) + attend(0, j)
        ).astype(BF)
        piece = x1_piece(j, x, c)
        for k in range(3):
            send(piece, piece, x1_x[j] + k, peers[k])
        send(piece, piece, x1_c[j] + 3, partner)

    def gather_states(j):
        for k in range(3):
            piece = x1_piece(j, wrap(x - k - 1, 4), c)
            arrive(piece, x1_x[j] + k)
            send(piece, piece, x1_c[j] + k, partner)

    def gather_states_wait(j):
        for k in range(3):
            arrive(x1_piece(j, wrap(x - k - 1, 4), other), x1_c[j] + k)
        arrive(x1_piece(j, x, other), x1_c[j] + 3)

    project(0, x0)
    phase_two(1, 1)
    step_states(1)
    phase_two(1, 2)
    arrive(kv.at[0, pl.ds(0, ROWS)], halo_f[0])
    step_states(0)
    gather_states(1)
    phase_two(1, 3)
    gather_states(0)
    gather_states_wait(1)
    gather_states_wait(0)
    phase_two(1, 4)
    project(1, x1)

    out_r = take("r", 2)

    def last_states(j):
        before_states = x1[j * ROWS:(j + 1) * ROWS, pl.ds(own_col, BLK)]
        x2[j * ROWS:(j + 1) * ROWS, :] = (before_states.astype(F32) + attend(1, j)).astype(BF)
        dst = outbuf.at[:, pl.ds(pl.multiple_of(xl * BLK, BLK), BLK)]
        src = x2.at[pl.ds(j * ROWS, ROWS)]
        send(src, dst, out_r + xl, dev(2 * yl + j, dest_y, z, c), away[j])

        @pl.when(home[j])
        def _():
            outbuf[:, pl.ds(pl.multiple_of(xl * BLK, BLK), BLK)] = x2[j * ROWS:(j + 1) * ROWS, :]

    last_states(1)
    arrive(kv.at[1, pl.ds(0, ROWS)], halo_f[1])
    last_states(0)
    for k in range(2):
        arrive(cotg.at[pl.ds(k * ROWS, ROWS)], a2a_c + k, away[k])

    def backward_segment(layer, j, grad_out):
        dq, dk, dv = [], [], []
        for h in range(2):
            cols = slice(h * HEAD, (h + 1) * HEAD)
            vcols = slice(BLK + h * HEAD, BLK + (h + 1) * HEAD)
            queries = q[layer, j * ROWS:(j + 1) * ROWS, cols]
            keys = kv[layer, j * ROWS:(j + 2) * ROWS, cols]
            values = kv[layer, j * ROWS:(j + 2) * ROWS, vcols]
            share = probs[layer, j, h]
            g = grad_out[:, cols]
            dp = nt(g, values)
            wide = share.astype(F32)
            r = jnp.sum(wide * dp, axis=-1, keepdims=True)
            ds = (wide * (dp - r) * SCALE).astype(BF)
            dq.append(nn(ds, keys))
            dk.append(tn(ds, queries))
            dv.append(tn(share, g))
        dqkv[j * ROWS:(j + 1) * ROWS, :BLK] = jnp.concatenate(dq, axis=1).astype(BF)
        return jnp.concatenate(dk + dv, axis=1)

    swap_r = [take("r", 2) for _ in range(LAYERS)]

    def project_back(layer, j):
        rows = slice(j * ROWS, (j + 1) * ROWS)
        lhs = dqkv[rows, :]
        for i in range(2):
            weight = w[layer, 2 * i + other].reshape(512, 3 * BLK)
            swap_send[layer, rows, i * 512:(i + 1) * 512] = nt(lhs, weight).astype(BF)
        src = swap_send.at[layer, pl.ds(j * ROWS, ROWS)]
        send(src, swap_recv.at[layer, pl.ds(j * ROWS, ROWS)], swap_r[layer] + j, partner)
        for i in range(2):
            weight = w[layer, 2 * i + c].reshape(512, 3 * BLK)
            own[rows, i * 512:(i + 1) * 512] = nt(lhs, weight)

    def back_layer(layer, grad_of):
        both = backward_segment(layer, 0, grad_of(0))
        halo_send[layer] = both[:ROWS].astype(BF)
        send(halo_send.at[layer], halo_recv.at[layer], halo_b[layer], group_dev(before))
        rest = both[ROWS:]
        both = backward_segment(layer, 1, grad_of(1))
        dqkv[:ROWS, BLK:] = (rest + both[:ROWS]).astype(BF)
        dkv[...] = both[ROWS:]
        project_back(layer, 0)
        arrive(halo_recv.at[layer], halo_b[layer])
        dqkv[ROWS:, BLK:] = (dkv[...] + halo_recv[layer].astype(F32)).astype(BF)
        project_back(layer, 1)

    back_layer(1, lambda j: cotg[j * ROWS:(j + 1) * ROWS, :])

    rs1_r = [take("r", 3) for _ in range(2)]
    mine = pl.multiple_of(x * BLK, BLK)
    for j in range(2):
        rows = slice(j * ROWS, (j + 1) * ROWS)
        arrive(swap_recv.at[1, pl.ds(j * ROWS, ROWS)], swap_r[1] + j)
        total = own[rows, :] + swap_recv[1, rows, :].astype(F32)
        own[rows, :] = total
        rs_send[1, rows, :] = total.astype(BF)
        for k in range(3):
            col = pl.multiple_of(wrap(x + k + 1, 4) * BLK, BLK)
            src = rs_send.at[1, pl.ds(j * ROWS, ROWS), pl.ds(col, BLK)]
            send(src, rs1_recv.at[k, pl.ds(j * ROWS, ROWS)], rs1_r[j] + k, peers[k])
        g1[rows, :] = cotg[rows, :].astype(F32) + own[rows, pl.ds(mine, BLK)]
    for j in range(2):
        rows = slice(j * ROWS, (j + 1) * ROWS)
        for k in range(3):
            arrive(rs1_recv.at[k, pl.ds(j * ROWS, ROWS)], rs1_r[j] + k)
        g1[rows, :] = (
            g1[rows, :] + rs1_recv[0, rows, :].astype(F32)
            + rs1_recv[1, rows, :].astype(F32) + rs1_recv[2, rows, :].astype(F32)
        )

    back_layer(0, lambda j: g1[j * ROWS:(j + 1) * ROWS, :].astype(BF))

    rs0_r = take("r", 4)
    for j in range(2):
        rows = slice(j * ROWS, (j + 1) * ROWS)
        own[rows, pl.ds(mine, BLK)] = own[rows, pl.ds(mine, BLK)] + g1[rows, :]
        arrive(swap_recv.at[0, pl.ds(j * ROWS, ROWS)], swap_r[0] + j)
        rs_send[0, rows, :] = (own[rows, :] + swap_recv[0, rows, :].astype(F32)).astype(BF)
        for half in range(2):
            src = rs_send.at[0, pl.ds(j * ROWS, ROWS), pl.ds(half * 512, 512)]
            here = (x == 2 * yl + j) & (yl == half)
            send(src, rs0_recv.at[x], rs0_r + x, dev(2 * yl + j, yh * 2 + half, z, c), jnp.logical_not(here))

            @pl.when(here)
            def _():
                rs0_recv[x] = rs_send[0, rows, half * 512:(half + 1) * 512]

    for k in range(2):
        arrive(outbuf.at[:, pl.ds(k * BLK, BLK)], out_r + k, away[k])
    out_ref[...] = outbuf[...]
    total = None
    for k in range(4):
        arrive(rs0_recv.at[k], rs0_r + k, jnp.logical_not(same & (x == k)))
    for k in range(4):
        term = rs0_recv[k].astype(F32)
        total = term if total is None else total + term
    grad_ref[...] = total

    for copy, cond in pending:
        if cond is None:
            copy.wait_send()
        else:
            pl.when(cond)(copy.wait_send)


def per_device(inputs, cotangent, w_query, w_key, w_value, boundary):
    vmem = pl.BlockSpec(memory_space=pltpu.VMEM)
    scratch = [
        ((2, LAYERS, 16, 3 * BLK), BF),
        ((LAYERS, 4, 8, 2, 2, 16, 3 * BLK), BF),
        ((GROUP_ROWS, D), BF),
        ((GROUP_ROWS, D), BF),
        ((GROUP_ROWS, BLK), BF),
        ((LAYERS, 3 * ROWS, 2 * BLK), BF),
        ((LAYERS, GROUP_ROWS, BLK), BF),
        ((LAYERS, 2, 2, ROWS, GROUP_ROWS), BF),
        ((ROWS, 2 * BLK), F32),
        ((LAYERS, ROWS, 2 * BLK), BF),
        ((LAYERS, ROWS, 2 * BLK), BF),
        ((GROUP_ROWS, 3 * BLK), BF),
        ((LAYERS, GROUP_ROWS, 1024), BF),
        ((LAYERS, GROUP_ROWS, 1024), BF),
        ((GROUP_ROWS, 1024), F32),
        ((LAYERS, GROUP_ROWS, 1024), BF),
        ((3, GROUP_ROWS, BLK), BF),
        ((4, ROWS, 512), BF),
        ((GROUP_ROWS, BLK), BF),
        ((ROWS, 512), BF),
        ((GROUP_ROWS, BLK), F32),
    ]
    return pl.pallas_call(
        kernel,
        out_shape=(
            jax.ShapeDtypeStruct((ROWS, 512), BF),
            jax.ShapeDtypeStruct((ROWS, 512), F32),
        ),
        in_specs=[vmem] * 5 + [pl.BlockSpec(memory_space=pltpu.SMEM)],
        out_specs=(vmem, vmem),
        scratch_shapes=[pltpu.VMEM(shape, kind) for shape, kind in scratch]
        + [pltpu.SemaphoreType.DMA((N_SEND,)), pltpu.SemaphoreType.DMA((N_RECV,))],
        compiler_params=pltpu.CompilerParams(
            collective_id=0, has_side_effects=True, vmem_limit_bytes=48 * 1024 * 1024
        ),
    )(inputs, cotangent, w_query, w_key, w_value, boundary)


def solution(mesh):
    return jax.shard_map(
        per_device,
        mesh=mesh,
        in_specs=(
            P("seg", "tp"),
            P("seg", "tp"),
            P(None, "seg", "tp"),
            P(None, "seg", "tp"),
            P(None, "seg", "tp"),
            P(),
        ),
        out_specs=(P("seg", "tp"), P("seg", "tp")),
        check_vma=False,
    )
```

```python
import math

import jax
import jax.numpy as jnp
from jax import lax
from jax.experimental import pallas as pl
from jax.experimental.pallas import tpu as pltpu
from jax.sharding import PartitionSpec as P

MESH = pl.DeviceIdType.MESH
HEAD = 128
LAYERS = 2
ROWS = 128
D = 2048
GROUP_ROWS = 2 * ROWS
BLK = 2 * HEAD
SCALE = 1.0 / math.sqrt(HEAD)
N_LOAD = 15
N_SEND = 36
N_RECV = 113
BF = jnp.bfloat16
F32 = jnp.float32


def nt(a, b):
    return lax.dot_general(a, b, (((1,), (1,)), ((), ())), preferred_element_type=F32)


def nn(a, b):
    return lax.dot_general(a, b, (((1,), (0,)), ((), ())), preferred_element_type=F32)


def tn(a, b):
    return lax.dot_general(a, b, (((0,), (0,)), ((), ())), preferred_element_type=F32)


def kernel(
    x_hbm, cot_hbm, wq, wk, wv, bound_hbm,
    out_ref, grad_ref,
    stage, w, x0, x1, cotg, kv, q, probs, dkv, dkv_last, halo_send, halo_recv, dqkv,
    swap_send, swap_recv, own, rs_send, rs1_recv, rs0_recv, x2, outbuf, g1,
    x_in, cot_in, bound, lsem, ssem, rsem,
):
    seg = lax.axis_index("seg")
    tp = lax.axis_index("tp")
    x = lax.rem(seg, 4)
    z = lax.rem(lax.div(seg, 4), 8)
    yh = lax.div(seg, 32)
    yl = lax.div(tp, 2)
    c = lax.rem(tp, 2)
    y = yh * 2 + yl
    other = 1 - c
    xh = lax.div(x, 2)
    xl = lax.rem(x, 2)

    def dev(dx, dy, dz, dc):
        return (lax.div(dy, 2) * 32 + dz * 4 + dx, lax.rem(dy, 2) * 2 + dc)

    def wrap(value, n):
        return lax.rem(value + n, n)

    me_y = y
    pair_y = yh * 2 + (1 - yl)
    group = yh * 16 + z * 2 + yl
    after = wrap(group + 1, 64)
    before = wrap(group - 1, 64)

    def group_dev(g):
        gy = lax.div(g, 16) * 2 + lax.rem(g, 2)
        return dev(x, gy, lax.rem(lax.div(g, 2), 8), c)

    partner = dev(x, y, z, other)
    peers = [dev(wrap(x + k, 4), y, z, c) for k in (1, 2, 3)]

    counts = {"s": 0, "r": 0}
    pending = []

    def take(kind, n=1):
        first = counts[kind]
        counts[kind] += n
        return first

    def batch(whole, cond=None):
        index = take("s")
        pending.append((whole, index, cond))
        return index

    def when(cond, action):
        if cond is None:
            action()
        else:
            pl.when(cond)(action)

    def send(src, dst, recv, target, cond=None, index=None):
        copy = pltpu.make_async_remote_copy(
            src_ref=src, dst_ref=dst, send_sem=ssem.at[batch(src, cond) if index is None else index],
            recv_sem=rsem.at[recv], device_id=target, device_id_type=MESH,
        )
        when(cond, copy.start)

    def arrive(dst, recv, cond=None):
        copy = pltpu.make_async_remote_copy(
            src_ref=dst, dst_ref=dst, send_sem=ssem.at[0], recv_sem=rsem.at[recv],
            device_id=partner, device_id_type=MESH,
        )
        when(cond, copy.wait_recv)

    loads = []

    def load(src, dst):
        copy = pltpu.make_async_copy(src, dst, lsem.at[len(loads)])
        copy.start()
        loads.append(copy)

    for layer in range(LAYERS):
        for j in range(2):
            for t, ref in enumerate((wq, wk, wv)):
                load(ref.at[layer, :, pl.ds(j * BLK, BLK)], stage.at[j, layer, :, pl.ds(t * BLK, BLK)])
    load(x_hbm, x_in)
    load(cot_hbm, cot_in)
    load(bound_hbm, bound)

    barrier = pltpu.get_barrier_semaphore()
    known = list(peers) + [partner, group_dev(after), group_dev(before)]
    known += [dev(wrap(x + k, 4), pair_y, z, c) for k in (1, 2, 3)]
    known += [dev(x, y, wrap(z + k, 8), c) for k in range(1, 8)]
    known += [dev(x, wrap(y + k, 8), z, c) for k in range(1, 8)]
    for device in known:
        pl.semaphore_signal(barrier, inc=1, device_id=device, device_id_type=MESH)
    for copy in loads:
        copy.wait()
    pl.semaphore_wait(barrier, len(known))

    same = xh == yl
    home = [same & (xl == j) for j in range(2)]
    away = [jnp.logical_not(h) for h in home]
    dest_y = yh * 2 + xh
    own_col = pl.multiple_of(xh * 1024 + c * 512 + xl * BLK, BLK)

    a2a_w = [take("r", 2) for _ in range(LAYERS)]
    a2a_c = take("r", 2)

    def spread_weights(layer):
        for j in range(2):
            dst = w.at[layer, yh, z, xh, xl]
            send(stage.at[j, layer], dst, a2a_w[layer] + xl, dev(2 * yl + j, dest_y, z, c), away[j])

            @pl.when(home[j])
            def _():
                w[layer, yh, z, xh, xl] = stage[j, layer]

    def spread_weights_wait(layer):
        for k in range(2):
            arrive(w.at[layer, yh, z, yl, k], a2a_w[layer] + k, away[k])

    spread_weights(0)
    spread_weights(1)

    x0_x = [[take("r") for _ in range(2)] for _ in range(2)]
    x0_c = take("r")
    x0_ring = batch(x0.at[:, pl.ds(0, 1536)], same)
    x0_pair = batch(x0.at[:, pl.ds(0, 1024)])
    my_rows = pl.multiple_of(xl * ROWS, ROWS)
    my_cols = pl.multiple_of(tp * 512, 512)

    @pl.when(same)
    def _():
        x0[pl.ds(my_rows, ROWS), pl.ds(my_cols, 512)] = x_in[...]

    send(
        x_in, x0.at[pl.ds(my_rows, ROWS), pl.ds(my_cols, 512)], x0_x[0][0] + xl * 2 + yl,
        dev(x, pair_y, z, c), jnp.logical_not(same),
    )

    def x0_piece(j, half, core):
        return x0.at[pl.ds(j * ROWS, ROWS), pl.ds(pl.multiple_of(half * 1024 + core * 512, 512), 512)]

    def x0_ring_send(j, half, local):
        piece = x0_piece(j, half, c)
        cond = home[j] & ((yl == half) if local else (yl != half))
        if not local:
            arrive(piece, x0_x[j][half], cond)
        for target in peers:
            send(piece, piece, x0_x[j][half], target, cond, x0_ring)

    def x0_swap(j, half):
        piece = x0_piece(j, half, c)
        arrive(piece, x0_x[j][half], away[j])
        send(piece, piece, x0_c, partner, None, x0_pair)

    def x0_all(action, *rest):
        for j in range(2):
            for half in range(2):
                action(j, half, *rest)

    x0_all(x0_ring_send, True)

    def spread_cotangent():
        for j in range(2):
            dst = cotg.at[pl.ds(my_rows, ROWS)]
            src = cot_in.at[:, pl.ds(j * BLK, BLK)]
            send(src, dst, a2a_c + xl, dev(2 * yl + j, dest_y, z, c), away[j])

            @pl.when(home[j])
            def _():
                cotg[pl.ds(my_rows, ROWS)] = cot_in[:, j * BLK:(j + 1) * BLK]

    out_z = 2 * lax.rem(z, 2) - 1
    out_y = 2 * yl - 1
    one = {(kind, rel): take("r") for kind in range(2) for rel in range(4)}
    direct = [take("r", 7) for _ in range(2)]

    def farthest(s, right):
        return 4 if (s == 0) == right else 3

    two = {
        (layer, kind, s, right, d): take("r")
        for layer in range(LAYERS) for kind in range(2) for s in range(2) for right in (False, True)
        for d in range(1, farthest(s, right) + 1)
    }

    next_to = [
        {k: dev(x, y, wrap(z + k, 8), c) for k in (1, -1)},
        {k: dev(x, wrap(y + k, 8), z, c) for k in (1, -1)},
    ]
    outer = [dev(x, y, wrap(z + out_z, 8), c), dev(x, wrap(y + out_y, 8), z, c)]
    mate = [dev(x, y, z - out_z, c), dev(x, y - out_y, z, c)]
    z_at = {k: wrap(z + k, 8) for k in range(-4, 5)}
    y_at = {k: (lax.div(wrap(y + k, 8), 2), lax.rem(wrap(y + k, 8), 2)) for k in range(-4, 5)}
    z_pair = lax.div(z, 2)
    pairs = [
        [z_pair * 2] + [wrap(z_pair + k, 4) * 2 for k in (out_z, -out_z, 2)],
        [yh] + [wrap(yh + k, 4) for k in (out_y, -out_y, 2)],
    ]

    def block(layer, kind, at_mate):
        if kind == 0:
            return w.at[layer, yh, z - out_z if at_mate else z, yl, 0]
        return w.at[layer, yh, z, 1 - yl if at_mate else yl, 1]

    def pair(layer, kind, rel, shift):
        if kind == 0:
            at = y_at[shift]
            return w.at[layer, at[0], pl.ds(pairs[0][rel], 2), at[1], 0]
        return w.at[layer, pairs[1][rel], z_at[shift], :, 1]

    def part(layer, kind, s, shift):
        if kind == 0:
            return w.at[layer, y_at[shift][0], pl.ds(4 * s, 4), y_at[shift][1], 0]
        return w.at[layer, pl.ds(2 * s, 2), z_at[shift], :, 1]

    batch_one = [[batch(w.at[layer, 0, pl.ds(0, 7), 0, 0]) for _ in range(2)] for layer in range(LAYERS)]
    batch_two = {
        (layer, kind, s): batch(w.at[layer, :, pl.ds(0, 6 if layer + kind + s == 0 else 7), 0, 0])
        for layer in range(LAYERS) for kind in range(2) for s in range(2)
    }
    lead = take("s")

    def pass_on(layer, kind, s, right, d):
        if d < farthest(s, right):
            piece = part(layer, kind, s, 0 if d == 0 else (-d if right else d))
            index = lead if right and layer + kind + s + d == 0 else batch_two[layer, kind, s]
            send(piece, piece, two[layer, kind, s, right, d + 1], next_to[1 - kind][1 if right else -1], None, index)

    def ring(layer, s, d):
        for kind in range(2):
            for right in (False, True):
                if 1 <= d <= farthest(s, right):
                    arrive(part(layer, kind, s, -d if right else d), two[layer, kind, s, right, d])
                if d <= farthest(s, right):
                    pass_on(layer, kind, s, right, d)

    def block_from(kind, k):
        if kind == 0:
            return w.at[0, yh, z_at[-k], yl, 0]
        return w.at[0, y_at[-k][0], z, y_at[-k][1], 1]

    def direct_send():
        for k in (1, -1, 2, -2, 3, -3, 4):
            for kind in range(2):
                mine = block(0, kind, False)
                to = wrap((z if kind == 0 else y) + k, 8)
                target = dev(x, y, to, c) if kind == 0 else dev(x, to, z, c)
                send(mine, mine, direct[kind] + k + 3 - (k > 0), target, None, batch_one[0][kind])

    def direct_wait():
        for k in (1, -1, 2, -2, 3, -3, 4):
            for kind in range(2):
                arrive(block_from(kind, k), direct[kind] + k + 3 - (k > 0))

    def relay(t):
        for kind in range(2):
            if t == 0:
                mine = block(1, kind, False)
                send(mine, mine, one[kind, 0], mate[kind], None, batch_one[1][kind])
                continue
            rel = t - 1
            if rel == 0:
                arrive(block(1, kind, True), one[kind, 0])
            else:
                arrive(pair(1, kind, rel, 0), one[kind, rel])
            if rel < 3:
                piece = pair(1, kind, rel, 0)
                send(piece, piece, one[kind, rel + 1], (mate if rel == 1 else outer)[kind], None, batch_one[1][kind])

    spread_weights_wait(0)
    direct_send()
    spread_weights_wait(1)
    relay(0)
    direct_wait()
    ring(0, 0, 0)
    x0_all(x0_ring_send, False)
    relay(1)
    head = part(0, 0, 0, 0)
    pltpu.make_async_remote_copy(
        src_ref=head, dst_ref=head, send_sem=ssem.at[lead], recv_sem=rsem.at[0],
        device_id=partner, device_id_type=MESH,
    ).wait_send()
    ring(0, 1, 0)
    ring(0, 0, 1)
    relay(2)
    ring(0, 1, 1)
    relay(3)
    ring(0, 0, 2)
    relay(4)
    ring(0, 1, 2)
    x0_all(x0_swap)
    ring(0, 0, 3)
    ring(1, 0, 0)
    ring(0, 1, 3)
    ring(1, 1, 0)
    spread_cotangent()
    ring(0, 0, 4)
    ring(0, 1, 4)
    arrive(x0.at[:, pl.ds(0, 1024)], x0_c)

    pos_q = lax.broadcasted_iota(jnp.int32, (ROWS, GROUP_ROWS), 0)
    pos_k = lax.broadcasted_iota(jnp.int32, (ROWS, GROUP_ROWS), 1)

    def mask(j):
        s = 2 * group + j
        now = bound[s]
        prev = bound[jnp.maximum(s - 1, 0)]
        first = jnp.where(prev == ROWS, 0, prev)
        first = jnp.where(s > 0, first, ROWS)
        pos_m = pos_k - ROWS
        memory = (pos_k < ROWS) & (pos_q < now) & (pos_k >= first)
        segment = (pos_m >= 0) & (pos_m <= pos_q) & ((pos_m >= now) | (pos_q < now))
        return memory | segment

    halo_f = [take("r") for _ in range(LAYERS)]
    halo_b = [take("r") for _ in range(LAYERS)]

    def project(layer, states):
        total = None
        for part in range(4):
            weight = w[layer, part].reshape(512, 3 * BLK)
            term = nn(states[:, part * 512:(part + 1) * 512], weight)
            total = term if total is None else total + term
        total = total.astype(BF)
        q[layer] = total[:, :BLK]
        kv[layer, ROWS:, :] = total[:, BLK:]
        tail = kv.at[layer, pl.ds(2 * ROWS, ROWS)]
        send(tail, kv.at[layer, pl.ds(0, ROWS)], halo_f[layer], group_dev(after))

    def attend(layer, j):
        visible = mask(j)
        results = []
        for h in range(2):
            cols = slice(h * HEAD, (h + 1) * HEAD)
            vcols = slice(BLK + h * HEAD, BLK + (h + 1) * HEAD)
            queries = q[layer, j * ROWS:(j + 1) * ROWS, cols]
            keys = kv[layer, j * ROWS:(j + 2) * ROWS, cols]
            values = kv[layer, j * ROWS:(j + 2) * ROWS, vcols]
            scores = jnp.where(visible, nt(queries, keys) * SCALE, -1e30)
            raised = jnp.exp(scores - jnp.max(scores, axis=-1, keepdims=True))
            share = (raised / jnp.sum(raised, axis=-1, keepdims=True)).astype(BF)
            probs[layer, j, h] = share
            results.append(nn(share, values))
        return jnp.concatenate(results, axis=1)

    def x1_piece(j, xs, core):
        col = lax.div(xs, 2) * 1024 + core * 512 + lax.rem(xs, 2) * BLK
        return x1.at[pl.ds(j * ROWS, ROWS), pl.ds(pl.multiple_of(col, BLK), BLK)]

    x1_x = [take("r", 3) for _ in range(2)]
    x1_c = take("r", 2)
    x1_sent = batch(x1.at[:, pl.ds(0, 1792)])

    def step_states(j):
        before_states = x0[j * ROWS:(j + 1) * ROWS, pl.ds(own_col, BLK)]
        x1[j * ROWS:(j + 1) * ROWS, pl.ds(own_col, BLK)] = (
            before_states.astype(F32) + attend(0, j)
        ).astype(BF)
        piece = x1_piece(j, x, c)
        for k in range(3):
            send(piece, piece, x1_x[j] + k, peers[k], None, x1_sent)
        send(piece, piece, x1_c + j, partner, None, x1_sent)

    def gather_states(j):
        for k in range(3):
            piece = x1_piece(j, wrap(x - k - 1, 4), c)
            arrive(piece, x1_x[j] + k)
            send(piece, piece, x1_c + j, partner, None, x1_sent)

    def gather_states_wait(j):
        arrive(x1.at[pl.ds(j * ROWS, ROWS), pl.ds(0, 1024)], x1_c + j)

    project(0, x0)
    ring(1, 0, 1)
    step_states(1)
    ring(1, 1, 1)
    arrive(kv.at[0, pl.ds(0, ROWS)], halo_f[0])
    step_states(0)
    ring(1, 0, 2)
    gather_states(1)
    ring(1, 1, 2)
    gather_states(0)
    ring(1, 0, 3)
    ring(1, 1, 3)
    gather_states_wait(1)
    gather_states_wait(0)
    ring(1, 0, 4)
    ring(1, 1, 4)
    project(1, x1)

    out_r = take("r", 2)

    def last_states(j):
        before_states = x1[j * ROWS:(j + 1) * ROWS, pl.ds(own_col, BLK)]
        x2[j * ROWS:(j + 1) * ROWS, :] = (before_states.astype(F32) + attend(1, j)).astype(BF)
        dst = outbuf.at[:, pl.ds(pl.multiple_of(xl * BLK, BLK), BLK)]
        src = x2.at[pl.ds(j * ROWS, ROWS)]
        send(src, dst, out_r + xl, dev(2 * yl + j, dest_y, z, c), away[j])

        @pl.when(home[j])
        def _():
            outbuf[:, pl.ds(pl.multiple_of(xl * BLK, BLK), BLK)] = x2[j * ROWS:(j + 1) * ROWS, :]

    def backward_segment(layer, j, grad_out):
        dq, dk, dv = [], [], []
        for h in range(2):
            cols = slice(h * HEAD, (h + 1) * HEAD)
            vcols = slice(BLK + h * HEAD, BLK + (h + 1) * HEAD)
            queries = q[layer, j * ROWS:(j + 1) * ROWS, cols]
            keys = kv[layer, j * ROWS:(j + 2) * ROWS, cols]
            values = kv[layer, j * ROWS:(j + 2) * ROWS, vcols]
            share = probs[layer, j, h]
            g = grad_out[:, cols]
            dp = nt(g, values)
            wide = share.astype(F32)
            r = jnp.sum(wide * dp, axis=-1, keepdims=True)
            ds = (wide * (dp - r) * SCALE).astype(BF)
            dq.append(nn(ds, keys))
            dk.append(tn(ds, queries))
            dv.append(tn(share, g))
        dqkv[j * ROWS:(j + 1) * ROWS, :BLK] = jnp.concatenate(dq, axis=1).astype(BF)
        return jnp.concatenate(dk + dv, axis=1)

    swap_r = [take("r", 2) for _ in range(LAYERS)]
    swap_sent = [batch(swap_send.at[layer]) for layer in range(LAYERS)]

    def project_back(layer, j):
        rows = slice(j * ROWS, (j + 1) * ROWS)
        lhs = dqkv[rows, :]
        for i in range(2):
            weight = w[layer, 2 * i + other].reshape(512, 3 * BLK)
            swap_send[layer, rows, i * 512:(i + 1) * 512] = nt(lhs, weight).astype(BF)
        src = swap_send.at[layer, pl.ds(j * ROWS, ROWS)]
        send(src, swap_recv.at[layer, pl.ds(j * ROWS, ROWS)], swap_r[layer] + j, partner, None, swap_sent[layer])
        for i in range(2):
            weight = w[layer, 2 * i + c].reshape(512, 3 * BLK)
            own[rows, i * 512:(i + 1) * 512] = nt(lhs, weight)

    def back_first(layer, grad):
        both = backward_segment(layer, 0, grad)
        halo_send[layer] = both[:ROWS].astype(BF)
        send(halo_send.at[layer], halo_recv.at[layer], halo_b[layer], group_dev(before))
        dkv[:ROWS, :] = both[ROWS:]

    def back_second(layer, grad):
        both = backward_segment(layer, 1, grad)
        dkv[ROWS:, :] = both[:ROWS]
        dkv_last[...] = both[ROWS:]

    def back_finish(layer):
        dqkv[:ROWS, BLK:] = (dkv[:ROWS, :] + dkv[ROWS:, :]).astype(BF)
        project_back(layer, 0)
        arrive(halo_recv.at[layer], halo_b[layer])
        dqkv[ROWS:, BLK:] = (dkv_last[...] + halo_recv[layer].astype(F32)).astype(BF)
        project_back(layer, 1)

    last_states(1)
    for k in range(2):
        arrive(cotg.at[pl.ds(k * ROWS, ROWS)], a2a_c + k, away[k])
    back_second(1, cotg[ROWS:, :])
    arrive(kv.at[1, pl.ds(0, ROWS)], halo_f[1])
    last_states(0)
    back_first(1, cotg[:ROWS, :])
    back_finish(1)

    rs1_r = take("r", 2)
    rs1_sent = batch(rs_send.at[1, :, pl.ds(0, 768)])
    mine = pl.multiple_of(x * BLK, BLK)
    for j in range(2):
        rows = slice(j * ROWS, (j + 1) * ROWS)
        arrive(swap_recv.at[1, pl.ds(j * ROWS, ROWS)], swap_r[1] + j)
        total = own[rows, :] + swap_recv[1, rows, :].astype(F32)
        own[rows, :] = total
        rs_send[1, rows, :] = total.astype(BF)
        for k in range(3):
            col = pl.multiple_of(wrap(x + k + 1, 4) * BLK, BLK)
            src = rs_send.at[1, pl.ds(j * ROWS, ROWS), pl.ds(col, BLK)]
            send(src, rs1_recv.at[k, pl.ds(j * ROWS, ROWS)], rs1_r + j, peers[k], None, rs1_sent)
        g1[rows, :] = cotg[rows, :].astype(F32) + own[rows, pl.ds(mine, BLK)]
    for j in range(2):
        rows = slice(j * ROWS, (j + 1) * ROWS)
        arrive(rs1_recv.at[:, pl.ds(j * ROWS, ROWS)], rs1_r + j)
        g1[rows, :] = (
            g1[rows, :] + rs1_recv[0, rows, :].astype(F32)
            + rs1_recv[1, rows, :].astype(F32) + rs1_recv[2, rows, :].astype(F32)
        )

    back_first(0, g1[:ROWS, :].astype(BF))
    back_second(0, g1[ROWS:, :].astype(BF))
    back_finish(0)

    rs0_r = take("r", 4)
    for j in range(2):
        rows = slice(j * ROWS, (j + 1) * ROWS)
        own[rows, pl.ds(mine, BLK)] = own[rows, pl.ds(mine, BLK)] + g1[rows, :]
        arrive(swap_recv.at[0, pl.ds(j * ROWS, ROWS)], swap_r[0] + j)
        rs_send[0, rows, :] = (own[rows, :] + swap_recv[0, rows, :].astype(F32)).astype(BF)
        for half in range(2):
            src = rs_send.at[0, pl.ds(j * ROWS, ROWS), pl.ds(half * 512, 512)]
            here = (x == 2 * yl + j) & (yl == half)
            send(src, rs0_recv.at[x], rs0_r + x, dev(2 * yl + j, yh * 2 + half, z, c), jnp.logical_not(here))

            @pl.when(here)
            def _():
                rs0_recv[x] = rs_send[0, rows, half * 512:(half + 1) * 512]

    for k in range(2):
        arrive(outbuf.at[:, pl.ds(k * BLK, BLK)], out_r + k, away[k])
    out_ref[...] = outbuf[...]
    total = None
    for k in range(4):
        arrive(rs0_recv.at[k], rs0_r + k, jnp.logical_not(same & (x == k)))
    for k in range(4):
        term = rs0_recv[k].astype(F32)
        total = term if total is None else total + term
    grad_ref[...] = total

    for whole, index, cond in pending:
        copy = pltpu.make_async_remote_copy(
            src_ref=whole, dst_ref=whole, send_sem=ssem.at[index], recv_sem=rsem.at[0],
            device_id=partner, device_id_type=MESH,
        )
        when(cond, copy.wait_send)

    assert counts["s"] <= N_SEND and counts["r"] <= N_RECV, counts


def per_device(inputs, cotangent, w_query, w_key, w_value, boundary):
    vmem = pl.BlockSpec(memory_space=pltpu.VMEM)
    scratch = [
        ((2, LAYERS, 16, 3 * BLK), BF),
        ((LAYERS, 4, 8, 2, 2, 16, 3 * BLK), BF),
        ((GROUP_ROWS, D), BF),
        ((GROUP_ROWS, D), BF),
        ((GROUP_ROWS, BLK), BF),
        ((LAYERS, 3 * ROWS, 2 * BLK), BF),
        ((LAYERS, GROUP_ROWS, BLK), BF),
        ((LAYERS, 2, 2, ROWS, GROUP_ROWS), BF),
        ((GROUP_ROWS, 2 * BLK), F32),
        ((ROWS, 2 * BLK), F32),
        ((LAYERS, ROWS, 2 * BLK), BF),
        ((LAYERS, ROWS, 2 * BLK), BF),
        ((GROUP_ROWS, 3 * BLK), BF),
        ((LAYERS, GROUP_ROWS, 1024), BF),
        ((LAYERS, GROUP_ROWS, 1024), BF),
        ((GROUP_ROWS, 1024), F32),
        ((LAYERS, GROUP_ROWS, 1024), BF),
        ((3, GROUP_ROWS, BLK), BF),
        ((4, ROWS, 512), BF),
        ((GROUP_ROWS, BLK), BF),
        ((ROWS, 512), BF),
        ((GROUP_ROWS, BLK), F32),
    ]
    return pl.pallas_call(
        kernel,
        out_shape=(
            jax.ShapeDtypeStruct((ROWS, 512), BF),
            jax.ShapeDtypeStruct((ROWS, 512), F32),
        ),
        in_specs=[pl.BlockSpec(memory_space=pl.ANY)] * 6,
        out_specs=(vmem, vmem),
        scratch_shapes=[pltpu.VMEM(shape, kind) for shape, kind in scratch]
        + [
            pltpu.VMEM((ROWS, 512), BF),
            pltpu.VMEM((ROWS, 512), BF),
            pltpu.SMEM((ROWS,), jnp.int32),
            pltpu.SemaphoreType.DMA((N_LOAD,)),
            pltpu.SemaphoreType.DMA((N_SEND,)), pltpu.SemaphoreType.DMA((N_RECV,)),
        ],
        compiler_params=pltpu.CompilerParams(
            collective_id=0, has_side_effects=True, vmem_limit_bytes=60 * 1024 * 1024
        ),
    )(inputs, cotangent, w_query, w_key, w_value, boundary)


def solution(mesh):
    return jax.shard_map(
        per_device,
        mesh=mesh,
        in_specs=(
            P("seg", "tp"),
            P("seg", "tp"),
            P(None, "seg", "tp"),
            P(None, "seg", "tp"),
            P(None, "seg", "tp"),
            P(),
        ),
        out_specs=(P("seg", "tp"), P("seg", "tp")),
        check_vma=False,
    )
```

```python
import math

import jax
import jax.numpy as jnp
from jax import lax
from jax.experimental import pallas as pl
from jax.experimental.pallas import tpu as pltpu
from jax.sharding import PartitionSpec as P

MESH = pl.DeviceIdType.MESH
HEAD = 128
LAYERS = 2
ROWS = 128
D = 2048
GROUP_ROWS = 2 * ROWS
BLK = 2 * HEAD
SCALE = 1.0 / math.sqrt(HEAD)
N_LOAD = 15
N_SEND = 36
N_RECV = 113
BF = jnp.bfloat16
F32 = jnp.float32


def nt(a, b):
    return lax.dot_general(a, b, (((1,), (1,)), ((), ())), preferred_element_type=F32)


def nn(a, b):
    return lax.dot_general(a, b, (((1,), (0,)), ((), ())), preferred_element_type=F32)


def tn(a, b):
    return lax.dot_general(a, b, (((0,), (0,)), ((), ())), preferred_element_type=F32)


def kernel(
    x_hbm, cot_hbm, wq, wk, wv, bound_hbm,
    out_ref, grad_ref,
    stage, w, x0, x1, cotg, kv, q, probs, dkv, dkv_last, halo_send, halo_recv, dqkv,
    swap_send, swap_recv, own, rs_send, rs1_recv, rs0_recv, x2, outbuf, g1,
    x_in, cot_in, bound, lsem, ssem, rsem,
):
    seg = lax.axis_index("seg")
    tp = lax.axis_index("tp")
    x = lax.rem(seg, 4)
    z = lax.rem(lax.div(seg, 4), 8)
    yh = lax.div(seg, 32)
    yl = lax.div(tp, 2)
    c = lax.rem(tp, 2)
    y = yh * 2 + yl
    other = 1 - c
    xh = lax.div(x, 2)
    xl = lax.rem(x, 2)

    def dev(dx, dy, dz, dc):
        return (lax.div(dy, 2) * 32 + dz * 4 + dx, lax.rem(dy, 2) * 2 + dc)

    def wrap(value, n):
        return lax.rem(value + n, n)

    me_y = y
    pair_y = yh * 2 + (1 - yl)
    group = yh * 16 + z * 2 + yl
    after = wrap(group + 1, 64)
    before = wrap(group - 1, 64)

    def group_dev(g):
        gy = lax.div(g, 16) * 2 + lax.rem(g, 2)
        return dev(x, gy, lax.rem(lax.div(g, 2), 8), c)

    partner = dev(x, y, z, other)
    peers = [dev(wrap(x + k, 4), y, z, c) for k in (1, 2, 3)]

    counts = {"s": 0, "r": 0}
    pending = []

    def take(kind, n=1):
        first = counts[kind]
        counts[kind] += n
        return first

    def batch(whole, cond=None):
        index = take("s")
        pending.append((whole, index, cond))
        return index

    def when(cond, action):
        if cond is None:
            action()
        else:
            pl.when(cond)(action)

    def send(src, dst, recv, target, cond=None, index=None):
        copy = pltpu.make_async_remote_copy(
            src_ref=src, dst_ref=dst, send_sem=ssem.at[batch(src, cond) if index is None else index],
            recv_sem=rsem.at[recv], device_id=target, device_id_type=MESH,
        )
        when(cond, copy.start)

    def arrive(dst, recv, cond=None):
        copy = pltpu.make_async_remote_copy(
            src_ref=dst, dst_ref=dst, send_sem=ssem.at[0], recv_sem=rsem.at[recv],
            device_id=partner, device_id_type=MESH,
        )
        when(cond, copy.wait_recv)

    loads = []

    def load(src, dst):
        copy = pltpu.make_async_copy(src, dst, lsem.at[len(loads)])
        copy.start()
        loads.append(copy)

    for layer in range(LAYERS):
        for j in range(2):
            for t, ref in enumerate((wq, wk, wv)):
                load(ref.at[layer, :, pl.ds(j * BLK, BLK)], stage.at[j, layer, :, pl.ds(t * BLK, BLK)])
    load(x_hbm, x_in)
    load(cot_hbm, cot_in)
    load(bound_hbm, bound)

    barrier = pltpu.get_barrier_semaphore()
    known = list(peers) + [partner, group_dev(after), group_dev(before)]
    known += [dev(wrap(x + k, 4), pair_y, z, c) for k in (1, 2, 3)]
    known += [dev(x, y, wrap(z + k, 8), c) for k in range(1, 8)]
    known += [dev(x, wrap(y + k, 8), z, c) for k in range(1, 8)]
    for device in known:
        pl.semaphore_signal(barrier, inc=1, device_id=device, device_id_type=MESH)
    for copy in loads:
        copy.wait()
    pl.semaphore_wait(barrier, len(known))

    same = xh == yl
    home = [same & (xl == j) for j in range(2)]
    away = [jnp.logical_not(h) for h in home]
    dest_y = yh * 2 + xh
    own_col = pl.multiple_of(xh * 1024 + c * 512 + xl * BLK, BLK)

    a2a_w = [take("r", 2) for _ in range(LAYERS)]
    a2a_c = take("r", 2)

    def spread_weights(layer):
        for j in range(2):
            dst = w.at[layer, yh, z, xh, xl]
            send(stage.at[j, layer], dst, a2a_w[layer] + xl, dev(2 * yl + j, dest_y, z, c), away[j])

            @pl.when(home[j])
            def _():
                w[layer, yh, z, xh, xl] = stage[j, layer]

    def spread_weights_wait(layer):
        for k in range(2):
            arrive(w.at[layer, yh, z, yl, k], a2a_w[layer] + k, away[k])

    spread_weights(0)
    spread_weights(1)

    x0_x = [[take("r") for _ in range(2)] for _ in range(2)]
    x0_c = take("r")
    x0_ring = batch(x0.at[:, pl.ds(0, 1536)], same)
    x0_pair = batch(x0.at[:, pl.ds(0, 1024)])
    my_rows = pl.multiple_of(xl * ROWS, ROWS)
    my_cols = pl.multiple_of(tp * 512, 512)

    @pl.when(same)
    def _():
        x0[pl.ds(my_rows, ROWS), pl.ds(my_cols, 512)] = x_in[...]

    send(
        x_in, x0.at[pl.ds(my_rows, ROWS), pl.ds(my_cols, 512)], x0_x[0][0] + xl * 2 + yl,
        dev(x, pair_y, z, c), jnp.logical_not(same),
    )

    def x0_piece(j, half, core):
        return x0.at[pl.ds(j * ROWS, ROWS), pl.ds(pl.multiple_of(half * 1024 + core * 512, 512), 512)]

    def x0_ring_send(j, half, local):
        piece = x0_piece(j, half, c)
        cond = home[j] & ((yl == half) if local else (yl != half))
        if not local:
            arrive(piece, x0_x[j][half], cond)
        for target in peers:
            send(piece, piece, x0_x[j][half], target, cond, x0_ring)

    def x0_swap(j, half):
        piece = x0_piece(j, half, c)
        arrive(piece, x0_x[j][half], away[j])
        send(piece, piece, x0_c, partner, None, x0_pair)

    def x0_all(action, *rest):
        for j in range(2):
            for half in range(2):
                action(j, half, *rest)

    x0_all(x0_ring_send, True)

    def spread_cotangent():
        for j in range(2):
            dst = cotg.at[pl.ds(my_rows, ROWS)]
            src = cot_in.at[:, pl.ds(j * BLK, BLK)]
            send(src, dst, a2a_c + xl, dev(2 * yl + j, dest_y, z, c), away[j])

            @pl.when(home[j])
            def _():
                cotg[pl.ds(my_rows, ROWS)] = cot_in[:, j * BLK:(j + 1) * BLK]

    out_z = 2 * lax.rem(z, 2) - 1
    out_y = 2 * yl - 1
    one = {(kind, rel): take("r") for kind in range(2) for rel in range(4)}
    direct = [take("r", 7) for _ in range(2)]

    def farthest(s, right):
        return 4 if (s == 0) == right else 3

    two = {
        (layer, kind, s, right, d): take("r")
        for layer in range(LAYERS) for kind in range(2) for s in range(2) for right in (False, True)
        for d in range(1, farthest(s, right) + 1)
    }

    next_to = [
        {k: dev(x, y, wrap(z + k, 8), c) for k in (1, -1)},
        {k: dev(x, wrap(y + k, 8), z, c) for k in (1, -1)},
    ]
    outer = [dev(x, y, wrap(z + out_z, 8), c), dev(x, wrap(y + out_y, 8), z, c)]
    mate = [dev(x, y, z - out_z, c), dev(x, y - out_y, z, c)]
    z_at = {k: wrap(z + k, 8) for k in range(-4, 5)}
    y_at = {k: (lax.div(wrap(y + k, 8), 2), lax.rem(wrap(y + k, 8), 2)) for k in range(-4, 5)}
    z_pair = lax.div(z, 2)
    pairs = [
        [z_pair * 2] + [wrap(z_pair + k, 4) * 2 for k in (out_z, -out_z, 2)],
        [yh] + [wrap(yh + k, 4) for k in (out_y, -out_y, 2)],
    ]

    def block(layer, kind, at_mate):
        if kind == 0:
            return w.at[layer, yh, z - out_z if at_mate else z, yl, 0]
        return w.at[layer, yh, z, 1 - yl if at_mate else yl, 1]

    def pair(layer, kind, rel, shift):
        if kind == 0:
            at = y_at[shift]
            return w.at[layer, at[0], pl.ds(pairs[0][rel], 2), at[1], 0]
        return w.at[layer, pairs[1][rel], z_at[shift], :, 1]

    def part(layer, kind, s, shift):
        if kind == 0:
            return w.at[layer, y_at[shift][0], pl.ds(4 * s, 4), y_at[shift][1], 0]
        return w.at[layer, pl.ds(2 * s, 2), z_at[shift], :, 1]

    batch_one = [[batch(w.at[layer, 0, pl.ds(0, 7), 0, 0]) for _ in range(2)] for layer in range(LAYERS)]
    batch_two = {
        (layer, kind, s): batch(w.at[layer, :, pl.ds(0, 6 if layer + kind + s == 0 else 7), 0, 0])
        for layer in range(LAYERS) for kind in range(2) for s in range(2)
    }
    lead = take("s")

    def pass_on(layer, kind, s, right, d):
        if d < farthest(s, right):
            piece = part(layer, kind, s, 0 if d == 0 else (-d if right else d))
            index = lead if right and layer + kind + s + d == 0 else batch_two[layer, kind, s]
            send(piece, piece, two[layer, kind, s, right, d + 1], next_to[1 - kind][1 if right else -1], None, index)

    def ring(layer, s, d):
        for kind in range(2):
            for right in (False, True):
                if 1 <= d <= farthest(s, right):
                    arrive(part(layer, kind, s, -d if right else d), two[layer, kind, s, right, d])
                if d <= farthest(s, right):
                    pass_on(layer, kind, s, right, d)

    def block_from(kind, k):
        if kind == 0:
            return w.at[0, yh, z_at[-k], yl, 0]
        return w.at[0, y_at[-k][0], z, y_at[-k][1], 1]

    def direct_send():
        for k in (1, -1, 2, -2, 3, -3, 4):
            for kind in range(2):
                mine = block(0, kind, False)
                to = wrap((z if kind == 0 else y) + k, 8)
                target = dev(x, y, to, c) if kind == 0 else dev(x, to, z, c)
                send(mine, mine, direct[kind] + k + 3 - (k > 0), target, None, batch_one[0][kind])

    def direct_wait():
        for k in (1, -1, 2, -2, 3, -3, 4):
            for kind in range(2):
                arrive(block_from(kind, k), direct[kind] + k + 3 - (k > 0))

    def relay(t):
        for kind in range(2):
            if t == 0:
                mine = block(1, kind, False)
                send(mine, mine, one[kind, 0], mate[kind], None, batch_one[1][kind])
                continue
            rel = t - 1
            if rel == 0:
                arrive(block(1, kind, True), one[kind, 0])
            else:
                arrive(pair(1, kind, rel, 0), one[kind, rel])
            if rel < 3:
                piece = pair(1, kind, rel, 0)
                send(piece, piece, one[kind, rel + 1], (mate if rel == 1 else outer)[kind], None, batch_one[1][kind])

    spread_weights_wait(0)
    direct_send()
    spread_weights_wait(1)
    relay(0)
    direct_wait()
    ring(0, 0, 0)
    x0_all(x0_ring_send, False)
    relay(1)
    head = part(0, 0, 0, 0)
    pltpu.make_async_remote_copy(
        src_ref=head, dst_ref=head, send_sem=ssem.at[lead], recv_sem=rsem.at[0],
        device_id=partner, device_id_type=MESH,
    ).wait_send()
    ring(0, 1, 0)
    ring(0, 0, 1)
    relay(2)
    ring(0, 1, 1)
    relay(3)
    ring(0, 0, 2)
    relay(4)
    ring(0, 1, 2)
    x0_all(x0_swap)
    ring(0, 0, 3)
    ring(1, 0, 0)
    ring(0, 1, 3)
    ring(1, 1, 0)
    spread_cotangent()
    ring(0, 0, 4)
    ring(0, 1, 4)
    arrive(x0.at[:, pl.ds(0, 1024)], x0_c)

    pos_q = lax.broadcasted_iota(jnp.int32, (ROWS, GROUP_ROWS), 0)
    pos_k = lax.broadcasted_iota(jnp.int32, (ROWS, GROUP_ROWS), 1)

    def mask(j):
        s = 2 * group + j
        now = bound[s]
        prev = bound[jnp.maximum(s - 1, 0)]
        first = jnp.where(prev == ROWS, 0, prev)
        first = jnp.where(s > 0, first, ROWS)
        pos_m = pos_k - ROWS
        memory = (pos_k < ROWS) & (pos_q < now) & (pos_k >= first)
        segment = (pos_m >= 0) & (pos_m <= pos_q) & ((pos_m >= now) | (pos_q < now))
        return memory | segment

    halo_f = [take("r") for _ in range(LAYERS)]
    halo_b = [take("r") for _ in range(LAYERS)]

    def project(layer, states):
        total = None
        for part in range(4):
            weight = w[layer, part].reshape(512, 3 * BLK)
            term = nn(states[:, part * 512:(part + 1) * 512], weight)
            total = term if total is None else total + term
        total = total.astype(BF)
        q[layer] = total[:, :BLK]
        kv[layer, ROWS:, :] = total[:, BLK:]
        tail = kv.at[layer, pl.ds(2 * ROWS, ROWS)]
        send(tail, kv.at[layer, pl.ds(0, ROWS)], halo_f[layer], group_dev(after))

    def attend(layer, j):
        visible = mask(j)
        results = []
        for h in range(2):
            cols = slice(h * HEAD, (h + 1) * HEAD)
            vcols = slice(BLK + h * HEAD, BLK + (h + 1) * HEAD)
            queries = q[layer, j * ROWS:(j + 1) * ROWS, cols]
            keys = kv[layer, j * ROWS:(j + 2) * ROWS, cols]
            values = kv[layer, j * ROWS:(j + 2) * ROWS, vcols]
            scores = jnp.where(visible, nt(queries, keys) * SCALE, -1e30)
            raised = jnp.exp(scores - jnp.max(scores, axis=-1, keepdims=True))
            share = (raised / jnp.sum(raised, axis=-1, keepdims=True)).astype(BF)
            probs[layer, j, h] = share
            results.append(nn(share, values))
        return jnp.concatenate(results, axis=1)

    def x1_piece(j, xs, core):
        col = lax.div(xs, 2) * 1024 + core * 512 + lax.rem(xs, 2) * BLK
        return x1.at[pl.ds(j * ROWS, ROWS), pl.ds(pl.multiple_of(col, BLK), BLK)]

    x1_x = [take("r", 3) for _ in range(2)]
    x1_c = take("r", 2)
    x1_sent = batch(x1.at[:, pl.ds(0, 1792)])

    def step_states(j):
        before_states = x0[j * ROWS:(j + 1) * ROWS, pl.ds(own_col, BLK)]
        x1[j * ROWS:(j + 1) * ROWS, pl.ds(own_col, BLK)] = (
            before_states.astype(F32) + attend(0, j)
        ).astype(BF)
        piece = x1_piece(j, x, c)
        for k in range(3):
            send(piece, piece, x1_x[j] + k, peers[k], None, x1_sent)
        send(piece, piece, x1_c + j, partner, None, x1_sent)

    def gather_states(j):
        for k in range(3):
            piece = x1_piece(j, wrap(x - k - 1, 4), c)
            arrive(piece, x1_x[j] + k)
            send(piece, piece, x1_c + j, partner, None, x1_sent)

    def gather_states_wait(j):
        arrive(x1.at[pl.ds(j * ROWS, ROWS), pl.ds(0, 1024)], x1_c + j)

    project(0, x0)
    ring(1, 0, 1)
    step_states(1)
    ring(1, 1, 1)
    arrive(kv.at[0, pl.ds(0, ROWS)], halo_f[0])
    step_states(0)
    ring(1, 0, 2)
    gather_states(1)
    ring(1, 1, 2)
    gather_states(0)
    ring(1, 0, 3)
    ring(1, 1, 3)
    gather_states_wait(1)
    gather_states_wait(0)
    ring(1, 0, 4)
    ring(1, 1, 4)
    project(1, x1)

    out_r = take("r", 2)

    def last_states(j):
        before_states = x1[j * ROWS:(j + 1) * ROWS, pl.ds(own_col, BLK)]
        x2[j * ROWS:(j + 1) * ROWS, :] = (before_states.astype(F32) + attend(1, j)).astype(BF)
        dst = outbuf.at[:, pl.ds(pl.multiple_of(xl * BLK, BLK), BLK)]
        src = x2.at[pl.ds(j * ROWS, ROWS)]
        send(src, dst, out_r + xl, dev(2 * yl + j, dest_y, z, c), away[j])

        @pl.when(home[j])
        def _():
            outbuf[:, pl.ds(pl.multiple_of(xl * BLK, BLK), BLK)] = x2[j * ROWS:(j + 1) * ROWS, :]

    def backward_segment(layer, j, grad_out):
        dq, dk, dv = [], [], []
        for h in range(2):
            cols = slice(h * HEAD, (h + 1) * HEAD)
            vcols = slice(BLK + h * HEAD, BLK + (h + 1) * HEAD)
            queries = q[layer, j * ROWS:(j + 1) * ROWS, cols]
            keys = kv[layer, j * ROWS:(j + 2) * ROWS, cols]
            values = kv[layer, j * ROWS:(j + 2) * ROWS, vcols]
            share = probs[layer, j, h]
            g = grad_out[:, cols]
            dp = nt(g, values)
            wide = share.astype(F32)
            r = jnp.sum(wide * dp, axis=-1, keepdims=True)
            ds = (wide * (dp - r) * SCALE).astype(BF)
            dq.append(nn(ds, keys))
            dk.append(tn(ds, queries))
            dv.append(tn(share, g))
        dqkv[j * ROWS:(j + 1) * ROWS, :BLK] = jnp.concatenate(dq, axis=1).astype(BF)
        return jnp.concatenate(dk + dv, axis=1)

    swap_r = [take("r", 2) for _ in range(LAYERS)]
    swap_sent = [batch(swap_send.at[layer]) for layer in range(LAYERS)]

    def project_back(layer, j):
        rows = slice(j * ROWS, (j + 1) * ROWS)
        lhs = dqkv[rows, :]
        for i in range(2):
            weight = w[layer, 2 * i + other].reshape(512, 3 * BLK)
            swap_send[layer, rows, i * 512:(i + 1) * 512] = nt(lhs, weight).astype(BF)
        src = swap_send.at[layer, pl.ds(j * ROWS, ROWS)]
        send(src, swap_recv.at[layer, pl.ds(j * ROWS, ROWS)], swap_r[layer] + j, partner, None, swap_sent[layer])
        for i in range(2):
            weight = w[layer, 2 * i + c].reshape(512, 3 * BLK)
            own[rows, i * 512:(i + 1) * 512] = nt(lhs, weight)

    def back_first(layer, grad):
        both = backward_segment(layer, 0, grad)
        halo_send[layer] = both[:ROWS].astype(BF)
        send(halo_send.at[layer], halo_recv.at[layer], halo_b[layer], group_dev(before))
        dkv[:ROWS, :] = both[ROWS:]

    def back_second(layer, grad):
        both = backward_segment(layer, 1, grad)
        dkv[ROWS:, :] = both[:ROWS]
        dkv_last[...] = both[ROWS:]

    rs1_r = take("r", 2)
    rs1_sent = batch(rs_send.at[1, :, pl.ds(0, 768)])
    rs0_r = take("r", 4)
    mine = pl.multiple_of(x * BLK, BLK)

    def swapped(layer, j):
        rows = slice(j * ROWS, (j + 1) * ROWS)
        arrive(swap_recv.at[layer, pl.ds(j * ROWS, ROWS)], swap_r[layer] + j)
        return own[rows, :] + swap_recv[layer, rows, :].astype(F32)

    def sum_one(j):
        rows = slice(j * ROWS, (j + 1) * ROWS)
        total = swapped(1, j)
        own[rows, :] = total
        rs_send[1, rows, :] = total.astype(BF)
        for k in range(3):
            col = pl.multiple_of(wrap(x + k + 1, 4) * BLK, BLK)
            src = rs_send.at[1, pl.ds(j * ROWS, ROWS), pl.ds(col, BLK)]
            send(src, rs1_recv.at[k, pl.ds(j * ROWS, ROWS)], rs1_r + j, peers[k], None, rs1_sent)
        g1[rows, :] = cotg[rows, :].astype(F32) + own[rows, pl.ds(mine, BLK)]

    def summed_one(j):
        rows = slice(j * ROWS, (j + 1) * ROWS)
        arrive(rs1_recv.at[:, pl.ds(j * ROWS, ROWS)], rs1_r + j)
        g1[rows, :] = (
            g1[rows, :] + rs1_recv[0, rows, :].astype(F32)
            + rs1_recv[1, rows, :].astype(F32) + rs1_recv[2, rows, :].astype(F32)
        )

    def sum_last(j):
        rows = slice(j * ROWS, (j + 1) * ROWS)
        own[rows, pl.ds(mine, BLK)] = own[rows, pl.ds(mine, BLK)] + g1[rows, :]
        rs_send[0, rows, :] = swapped(0, j).astype(BF)
        for half in range(2):
            src = rs_send.at[0, pl.ds(j * ROWS, ROWS), pl.ds(half * 512, 512)]
            here = (x == 2 * yl + j) & (yl == half)
            send(src, rs0_recv.at[x], rs0_r + x, dev(2 * yl + j, yh * 2 + half, z, c), jnp.logical_not(here))

            @pl.when(here)
            def _():
                rs0_recv[x] = rs_send[0, rows, half * 512:(half + 1) * 512]

    def back_own(layer):
        dqkv[:ROWS, BLK:] = (dkv[:ROWS, :] + dkv[ROWS:, :]).astype(BF)
        project_back(layer, 0)

    def back_halo(layer):
        arrive(halo_recv.at[layer], halo_b[layer])
        dqkv[ROWS:, BLK:] = (dkv_last[...] + halo_recv[layer].astype(F32)).astype(BF)
        project_back(layer, 1)

    last_states(1)
    for k in range(2):
        arrive(cotg.at[pl.ds(k * ROWS, ROWS)], a2a_c + k, away[k])
    back_second(1, cotg[ROWS:, :])
    arrive(kv.at[1, pl.ds(0, ROWS)], halo_f[1])
    last_states(0)
    back_first(1, cotg[:ROWS, :])
    back_own(1)
    sum_one(0)
    back_halo(1)
    sum_one(1)
    summed_one(0)
    back_first(0, g1[:ROWS, :].astype(BF))
    summed_one(1)
    back_second(0, g1[ROWS:, :].astype(BF))
    back_own(0)
    back_halo(0)
    sum_last(0)
    sum_last(1)

    for k in range(2):
        arrive(outbuf.at[:, pl.ds(k * BLK, BLK)], out_r + k, away[k])
    out_ref[...] = outbuf[...]
    total = None
    for k in range(4):
        arrive(rs0_recv.at[k], rs0_r + k, jnp.logical_not(same & (x == k)))
    for k in range(4):
        term = rs0_recv[k].astype(F32)
        total = term if total is None else total + term
    grad_ref[...] = total

    for whole, index, cond in pending:
        copy = pltpu.make_async_remote_copy(
            src_ref=whole, dst_ref=whole, send_sem=ssem.at[index], recv_sem=rsem.at[0],
            device_id=partner, device_id_type=MESH,
        )
        when(cond, copy.wait_send)

    assert counts["s"] <= N_SEND and counts["r"] <= N_RECV, counts


def per_device(inputs, cotangent, w_query, w_key, w_value, boundary):
    vmem = pl.BlockSpec(memory_space=pltpu.VMEM)
    scratch = [
        ((2, LAYERS, 16, 3 * BLK), BF),
        ((LAYERS, 4, 8, 2, 2, 16, 3 * BLK), BF),
        ((GROUP_ROWS, D), BF),
        ((GROUP_ROWS, D), BF),
        ((GROUP_ROWS, BLK), BF),
        ((LAYERS, 3 * ROWS, 2 * BLK), BF),
        ((LAYERS, GROUP_ROWS, BLK), BF),
        ((LAYERS, 2, 2, ROWS, GROUP_ROWS), BF),
        ((GROUP_ROWS, 2 * BLK), F32),
        ((ROWS, 2 * BLK), F32),
        ((LAYERS, ROWS, 2 * BLK), BF),
        ((LAYERS, ROWS, 2 * BLK), BF),
        ((GROUP_ROWS, 3 * BLK), BF),
        ((LAYERS, GROUP_ROWS, 1024), BF),
        ((LAYERS, GROUP_ROWS, 1024), BF),
        ((GROUP_ROWS, 1024), F32),
        ((LAYERS, GROUP_ROWS, 1024), BF),
        ((3, GROUP_ROWS, BLK), BF),
        ((4, ROWS, 512), BF),
        ((GROUP_ROWS, BLK), BF),
        ((ROWS, 512), BF),
        ((GROUP_ROWS, BLK), F32),
    ]
    return pl.pallas_call(
        kernel,
        out_shape=(
            jax.ShapeDtypeStruct((ROWS, 512), BF),
            jax.ShapeDtypeStruct((ROWS, 512), F32),
        ),
        in_specs=[pl.BlockSpec(memory_space=pl.ANY)] * 6,
        out_specs=(vmem, vmem),
        scratch_shapes=[pltpu.VMEM(shape, kind) for shape, kind in scratch]
        + [
            pltpu.VMEM((ROWS, 512), BF),
            pltpu.VMEM((ROWS, 512), BF),
            pltpu.SMEM((ROWS,), jnp.int32),
            pltpu.SemaphoreType.DMA((N_LOAD,)),
            pltpu.SemaphoreType.DMA((N_SEND,)), pltpu.SemaphoreType.DMA((N_RECV,)),
        ],
        compiler_params=pltpu.CompilerParams(
            collective_id=0, has_side_effects=True, vmem_limit_bytes=60 * 1024 * 1024
        ),
    )(inputs, cotangent, w_query, w_key, w_value, boundary)


def solution(mesh):
    return jax.shard_map(
        per_device,
        mesh=mesh,
        in_specs=(
            P("seg", "tp"),
            P("seg", "tp"),
            P(None, "seg", "tp"),
            P(None, "seg", "tp"),
            P(None, "seg", "tp"),
            P(),
        ),
        out_specs=(P("seg", "tp"), P("seg", "tp")),
        check_vma=False,
    )
```

```python
import math

import jax
import jax.numpy as jnp
from jax import lax
from jax.experimental import pallas as pl
from jax.experimental.pallas import tpu as pltpu
from jax.sharding import PartitionSpec as P

MESH = pl.DeviceIdType.MESH
HEAD = 128
LAYERS = 2
ROWS = 128
D = 2048
GROUP_ROWS = 2 * ROWS
BLK = 2 * HEAD
SCALE = 1.0 / math.sqrt(HEAD)
N_LOAD = 15
N_SEND = 36
N_RECV = 117
BF = jnp.bfloat16
F32 = jnp.float32


def nt(a, b):
    return lax.dot_general(a, b, (((1,), (1,)), ((), ())), preferred_element_type=F32)


def nn(a, b):
    return lax.dot_general(a, b, (((1,), (0,)), ((), ())), preferred_element_type=F32)


def tn(a, b):
    return lax.dot_general(a, b, (((0,), (0,)), ((), ())), preferred_element_type=F32)


def kernel(
    x_hbm, cot_hbm, wq, wk, wv, bound_hbm,
    out_ref, grad_ref,
    stage, w, x0, x1, cotg, kv, q, probs, dkv, dkv_last, halo_send, halo_recv, dqkv,
    swap_send, swap_recv, own, rs_send, rs1_recv, rs0_recv, x2, outbuf, g1,
    x_in, cot_in, bound, lsem, ssem, rsem,
):
    seg = lax.axis_index("seg")
    tp = lax.axis_index("tp")
    x = lax.rem(seg, 4)
    z = lax.rem(lax.div(seg, 4), 8)
    yh = lax.div(seg, 32)
    yl = lax.div(tp, 2)
    c = lax.rem(tp, 2)
    y = yh * 2 + yl
    other = 1 - c
    xh = lax.div(x, 2)
    xl = lax.rem(x, 2)

    def dev(dx, dy, dz, dc):
        return (lax.div(dy, 2) * 32 + dz * 4 + dx, lax.rem(dy, 2) * 2 + dc)

    def wrap(value, n):
        return lax.rem(value + n, n)

    me_y = y
    pair_y = yh * 2 + (1 - yl)
    group = yh * 16 + z * 2 + yl
    after = wrap(group + 1, 64)
    before = wrap(group - 1, 64)

    def group_dev(g):
        gy = lax.div(g, 16) * 2 + lax.rem(g, 2)
        return dev(x, gy, lax.rem(lax.div(g, 2), 8), c)

    partner = dev(x, y, z, other)
    peers = [dev(wrap(x + k, 4), y, z, c) for k in (1, 2, 3)]

    counts = {"s": 0, "r": 0}
    pending = []

    def take(kind, n=1):
        first = counts[kind]
        counts[kind] += n
        return first

    def batch(whole, cond=None):
        index = take("s")
        pending.append((whole, index, cond))
        return index

    def when(cond, action):
        if cond is None:
            action()
        else:
            pl.when(cond)(action)

    def send(src, dst, recv, target, cond=None, index=None):
        copy = pltpu.make_async_remote_copy(
            src_ref=src, dst_ref=dst, send_sem=ssem.at[batch(src, cond) if index is None else index],
            recv_sem=rsem.at[recv], device_id=target, device_id_type=MESH,
        )
        when(cond, copy.start)

    def arrive(dst, recv, cond=None):
        copy = pltpu.make_async_remote_copy(
            src_ref=dst, dst_ref=dst, send_sem=ssem.at[0], recv_sem=rsem.at[recv],
            device_id=partner, device_id_type=MESH,
        )
        when(cond, copy.wait_recv)

    loads = []

    def load(src, dst):
        copy = pltpu.make_async_copy(src, dst, lsem.at[len(loads)])
        copy.start()
        loads.append(copy)

    for layer in range(LAYERS):
        for j in range(2):
            for t, ref in enumerate((wq, wk, wv)):
                load(ref.at[layer, :, pl.ds(j * BLK, BLK)], stage.at[j, layer, :, pl.ds(t * BLK, BLK)])
    load(x_hbm, x_in)
    load(cot_hbm, cot_in)
    load(bound_hbm, bound)

    barrier = pltpu.get_barrier_semaphore()
    known = list(peers) + [partner, group_dev(after), group_dev(before)]
    known += [dev(wrap(x + k, 4), pair_y, z, c) for k in (1, 2, 3)]
    known += [dev(x, y, wrap(z + k, 8), c) for k in range(1, 8)]
    known += [dev(x, wrap(y + k, 8), z, c) for k in range(1, 8)]
    for device in known:
        pl.semaphore_signal(barrier, inc=1, device_id=device, device_id_type=MESH)
    for copy in loads:
        copy.wait()
    pl.semaphore_wait(barrier, len(known))

    same = xh == yl
    home = [same & (xl == j) for j in range(2)]
    away = [jnp.logical_not(h) for h in home]
    dest_y = yh * 2 + xh
    own_col = pl.multiple_of(xh * 1024 + c * 512 + xl * BLK, BLK)

    a2a_w = [take("r", 2) for _ in range(LAYERS)]
    a2a_c = take("r", 2)

    def spread_weights(layer):
        for j in range(2):
            dst = w.at[layer, yh, z, xh, xl]
            send(stage.at[j, layer], dst, a2a_w[layer] + xl, dev(2 * yl + j, dest_y, z, c), away[j])

            @pl.when(home[j])
            def _():
                w[layer, yh, z, xh, xl] = stage[j, layer]

    def spread_weights_wait(layer):
        for k in range(2):
            arrive(w.at[layer, yh, z, yl, k], a2a_w[layer] + k, away[k])

    spread_weights(0)
    spread_weights(1)

    x0_x = [[take("r") for _ in range(2)] for _ in range(2)]
    x0_c = take("r")
    x0_ring = batch(x0.at[pl.ds(0, GROUP_ROWS), pl.ds(0, 1536)], same)
    x0_pair = batch(x0.at[pl.ds(0, GROUP_ROWS), pl.ds(0, 1024)])
    last_r, last_x, last_c = take("r", LAYERS), take("r", LAYERS), take("r", LAYERS)
    last_sent = [batch(x0.at[pl.ds(0, GROUP_ROWS), pl.ds(0, 1024)]) for _ in range(LAYERS)]
    states_of = (x0, x1)
    my_rows = pl.multiple_of(xl * ROWS, ROWS)
    my_cols = pl.multiple_of(tp * 512, 512)

    @pl.when(same)
    def _():
        x0[pl.ds(ROWS + my_rows, ROWS), pl.ds(my_cols, 512)] = x_in[...]

    send(
        x_in, x0.at[pl.ds(ROWS + my_rows, ROWS), pl.ds(my_cols, 512)], x0_x[0][0] + xl * 2 + yl,
        dev(x, pair_y, z, c), jnp.logical_not(same),
    )

    def x0_piece(j, half, core):
        return x0.at[pl.ds((j + 1) * ROWS, ROWS), pl.ds(pl.multiple_of(half * 1024 + core * 512, 512), 512)]

    def x0_ring_send(j, half, local):
        piece = x0_piece(j, half, c)
        cond = home[j] & ((yl == half) if local else (yl != half))
        if not local:
            arrive(piece, x0_x[j][half], cond)
        for target in peers:
            send(piece, piece, x0_x[j][half], target, cond, x0_ring)

    def x0_swap(j, half):
        piece = x0_piece(j, half, c)
        arrive(piece, x0_x[j][half], away[j])
        send(piece, piece, x0_c, partner, None, x0_pair)

    def x0_all(action, *rest):
        for j in range(2):
            for half in range(2):
                action(j, half, *rest)

    x0_all(x0_ring_send, True)

    def quarter(layer, row, xs, core):
        col = lax.div(xs, 2) * 1024 + core * 512 + lax.rem(xs, 2) * BLK
        return states_of[layer].at[pl.ds(row, ROWS), pl.ds(pl.multiple_of(col, BLK), BLK)]

    def last_send(layer):
        piece, dst = quarter(layer, 2 * ROWS, x, c), quarter(layer, 0, x, c)
        send(piece, dst, last_r + layer, group_dev(after), None, last_sent[layer])

    def last_spread(layer):
        piece = quarter(layer, 0, x, c)
        arrive(piece, last_r + layer)
        for target in peers:
            send(piece, piece, last_x + layer, target, None, last_sent[layer])
        send(piece, piece, last_c + layer, partner, None, last_sent[layer])

    def last_swap(layer):
        arrive(states_of[layer].at[pl.ds(0, ROWS), pl.ds(0, 768)], last_x + layer)
        for k in range(3):
            piece = quarter(layer, 0, wrap(x - k - 1, 4), c)
            send(piece, piece, last_c + layer, partner, None, last_sent[layer])

    def last_wait(layer):
        arrive(states_of[layer].at[pl.ds(0, ROWS), pl.ds(0, 1024)], last_c + layer)

    def spread_cotangent():
        for j in range(2):
            dst = cotg.at[pl.ds(my_rows, ROWS)]
            src = cot_in.at[:, pl.ds(j * BLK, BLK)]
            send(src, dst, a2a_c + xl, dev(2 * yl + j, dest_y, z, c), away[j])

            @pl.when(home[j])
            def _():
                cotg[pl.ds(my_rows, ROWS)] = cot_in[:, j * BLK:(j + 1) * BLK]

    out_z = 2 * lax.rem(z, 2) - 1
    out_y = 2 * yl - 1
    one = {(kind, rel): take("r") for kind in range(2) for rel in range(4)}
    direct = [take("r", 7) for _ in range(2)]

    def farthest(s, right):
        return 4 if (s == 0) == right else 3

    two = {
        (layer, kind, s, right, d): take("r")
        for layer in range(LAYERS) for kind in range(2) for s in range(2) for right in (False, True)
        for d in range(1, farthest(s, right) + 1)
    }

    next_to = [
        {k: dev(x, y, wrap(z + k, 8), c) for k in (1, -1)},
        {k: dev(x, wrap(y + k, 8), z, c) for k in (1, -1)},
    ]
    outer = [dev(x, y, wrap(z + out_z, 8), c), dev(x, wrap(y + out_y, 8), z, c)]
    mate = [dev(x, y, z - out_z, c), dev(x, y - out_y, z, c)]
    z_at = {k: wrap(z + k, 8) for k in range(-4, 5)}
    y_at = {k: (lax.div(wrap(y + k, 8), 2), lax.rem(wrap(y + k, 8), 2)) for k in range(-4, 5)}
    z_pair = lax.div(z, 2)
    pairs = [
        [z_pair * 2] + [wrap(z_pair + k, 4) * 2 for k in (out_z, -out_z, 2)],
        [yh] + [wrap(yh + k, 4) for k in (out_y, -out_y, 2)],
    ]

    def block(layer, kind, at_mate):
        if kind == 0:
            return w.at[layer, yh, z - out_z if at_mate else z, yl, 0]
        return w.at[layer, yh, z, 1 - yl if at_mate else yl, 1]

    def pair(layer, kind, rel, shift):
        if kind == 0:
            at = y_at[shift]
            return w.at[layer, at[0], pl.ds(pairs[0][rel], 2), at[1], 0]
        return w.at[layer, pairs[1][rel], z_at[shift], :, 1]

    def part(layer, kind, s, shift):
        if kind == 0:
            return w.at[layer, y_at[shift][0], pl.ds(4 * s, 4), y_at[shift][1], 0]
        return w.at[layer, pl.ds(2 * s, 2), z_at[shift], :, 1]

    batch_one = [[batch(w.at[layer, 0, pl.ds(0, 7), 0, 0]) for _ in range(2)] for layer in range(LAYERS)]
    batch_two = {
        (layer, kind, s): batch(w.at[layer, :, pl.ds(0, 6 if layer + kind + s == 0 else 7), 0, 0])
        for layer in range(LAYERS) for kind in range(2) for s in range(2)
    }
    lead = take("s")

    def pass_on(layer, kind, s, right, d):
        if d < farthest(s, right):
            piece = part(layer, kind, s, 0 if d == 0 else (-d if right else d))
            index = lead if right and layer + kind + s + d == 0 else batch_two[layer, kind, s]
            send(piece, piece, two[layer, kind, s, right, d + 1], next_to[1 - kind][1 if right else -1], None, index)

    def ring(layer, s, d):
        for kind in range(2):
            for right in (False, True):
                if 1 <= d <= farthest(s, right):
                    arrive(part(layer, kind, s, -d if right else d), two[layer, kind, s, right, d])
                if d <= farthest(s, right):
                    pass_on(layer, kind, s, right, d)

    def block_from(kind, k):
        if kind == 0:
            return w.at[0, yh, z_at[-k], yl, 0]
        return w.at[0, y_at[-k][0], z, y_at[-k][1], 1]

    def direct_send():
        for k in (1, -1, 2, -2, 3, -3, 4):
            for kind in range(2):
                mine = block(0, kind, False)
                to = wrap((z if kind == 0 else y) + k, 8)
                target = dev(x, y, to, c) if kind == 0 else dev(x, to, z, c)
                send(mine, mine, direct[kind] + k + 3 - (k > 0), target, None, batch_one[0][kind])

    def direct_wait():
        for k in (1, -1, 2, -2, 3, -3, 4):
            for kind in range(2):
                arrive(block_from(kind, k), direct[kind] + k + 3 - (k > 0))

    def relay(t):
        for kind in range(2):
            if t == 0:
                mine = block(1, kind, False)
                send(mine, mine, one[kind, 0], mate[kind], None, batch_one[1][kind])
                continue
            rel = t - 1
            if rel == 0:
                arrive(block(1, kind, True), one[kind, 0])
            else:
                arrive(pair(1, kind, rel, 0), one[kind, rel])
            if rel < 3:
                piece = pair(1, kind, rel, 0)
                send(piece, piece, one[kind, rel + 1], (mate if rel == 1 else outer)[kind], None, batch_one[1][kind])

    spread_weights_wait(0)
    direct_send()
    spread_weights_wait(1)
    relay(0)
    direct_wait()
    ring(0, 0, 0)
    x0_all(x0_ring_send, False)
    relay(1)
    head = part(0, 0, 0, 0)
    pltpu.make_async_remote_copy(
        src_ref=head, dst_ref=head, send_sem=ssem.at[lead], recv_sem=rsem.at[0],
        device_id=partner, device_id_type=MESH,
    ).wait_send()
    ring(0, 1, 0)
    ring(0, 0, 1)
    relay(2)
    x0_all(x0_swap)
    last_send(0)
    ring(0, 1, 1)
    relay(3)
    ring(0, 0, 2)
    relay(4)
    ring(0, 1, 2)
    last_spread(0)
    ring(0, 0, 3)
    ring(1, 0, 0)
    ring(0, 1, 3)
    ring(1, 1, 0)
    last_swap(0)
    spread_cotangent()
    ring(0, 0, 4)
    ring(0, 1, 4)
    arrive(x0.at[pl.ds(0, GROUP_ROWS), pl.ds(0, 1024)], x0_c)
    last_wait(0)

    pos_q = lax.broadcasted_iota(jnp.int32, (ROWS, GROUP_ROWS), 0)
    pos_k = lax.broadcasted_iota(jnp.int32, (ROWS, GROUP_ROWS), 1)

    def mask(j):
        s = 2 * group + j
        now = bound[s]
        prev = bound[jnp.maximum(s - 1, 0)]
        first = jnp.where(prev == ROWS, 0, prev)
        first = jnp.where(s > 0, first, ROWS)
        pos_m = pos_k - ROWS
        memory = (pos_k < ROWS) & (pos_q < now) & (pos_k >= first)
        segment = (pos_m >= 0) & (pos_m <= pos_q) & ((pos_m >= now) | (pos_q < now))
        return memory | segment

    halo_b = [take("r") for _ in range(LAYERS)]

    def project(layer, states):
        def columns(first, last):
            total = None
            for part in range(4):
                weight = w[layer, part].reshape(512, 3 * BLK)[:, first:last]
                rows = slice(0 if first else ROWS, None)
                term = nn(states[rows, part * 512:(part + 1) * 512], weight)
                total = term if total is None else total + term
            return total.astype(BF)

        kv[layer] = columns(BLK, 3 * BLK)
        q[layer] = columns(0, BLK)

    def attend(layer, j):
        visible = mask(j)
        results = []
        for h in range(2):
            cols = slice(h * HEAD, (h + 1) * HEAD)
            vcols = slice(BLK + h * HEAD, BLK + (h + 1) * HEAD)
            queries = q[layer, j * ROWS:(j + 1) * ROWS, cols]
            keys = kv[layer, j * ROWS:(j + 2) * ROWS, cols]
            values = kv[layer, j * ROWS:(j + 2) * ROWS, vcols]
            scores = jnp.where(visible, nt(queries, keys) * SCALE, -1e30)
            raised = jnp.exp(scores - jnp.max(scores, axis=-1, keepdims=True))
            share = (raised / jnp.sum(raised, axis=-1, keepdims=True)).astype(BF)
            probs[layer, j, h] = share
            results.append(nn(share, values))
        return jnp.concatenate(results, axis=1)

    def x1_piece(j, xs, core):
        return quarter(1, (j + 1) * ROWS, xs, core)

    x1_x = [take("r", 3) for _ in range(2)]
    x1_c = take("r", 2)
    x1_sent = batch(x1.at[pl.ds(0, GROUP_ROWS), pl.ds(0, 1792)])

    def step_states(j):
        before_states = x0[(j + 1) * ROWS:(j + 2) * ROWS, pl.ds(own_col, BLK)]
        x1[(j + 1) * ROWS:(j + 2) * ROWS, pl.ds(own_col, BLK)] = (
            before_states.astype(F32) + attend(0, j)
        ).astype(BF)
        piece = x1_piece(j, x, c)
        for k in range(3):
            send(piece, piece, x1_x[j] + k, peers[k], None, x1_sent)
        send(piece, piece, x1_c + j, partner, None, x1_sent)

    def gather_states(j):
        for k in range(3):
            piece = x1_piece(j, wrap(x - k - 1, 4), c)
            arrive(piece, x1_x[j] + k)
            send(piece, piece, x1_c + j, partner, None, x1_sent)

    def gather_states_wait(j):
        arrive(x1.at[pl.ds((j + 1) * ROWS, ROWS), pl.ds(0, 1024)], x1_c + j)

    project(0, x0)
    ring(1, 0, 1)
    step_states(1)
    last_send(1)
    ring(1, 1, 1)
    step_states(0)
    ring(1, 0, 2)
    gather_states(1)
    ring(1, 1, 2)
    last_spread(1)
    gather_states(0)
    ring(1, 0, 3)
    ring(1, 1, 3)
    last_swap(1)
    gather_states_wait(1)
    gather_states_wait(0)
    ring(1, 0, 4)
    ring(1, 1, 4)
    last_wait(1)
    project(1, x1)

    out_r = take("r", 2)

    def last_states(j):
        before_states = x1[(j + 1) * ROWS:(j + 2) * ROWS, pl.ds(own_col, BLK)]
        x2[j * ROWS:(j + 1) * ROWS, :] = (before_states.astype(F32) + attend(1, j)).astype(BF)
        dst = outbuf.at[:, pl.ds(pl.multiple_of(xl * BLK, BLK), BLK)]
        src = x2.at[pl.ds(j * ROWS, ROWS)]
        send(src, dst, out_r + xl, dev(2 * yl + j, dest_y, z, c), away[j])

        @pl.when(home[j])
        def _():
            outbuf[:, pl.ds(pl.multiple_of(xl * BLK, BLK), BLK)] = x2[j * ROWS:(j + 1) * ROWS, :]

    def backward_segment(layer, j, grad_out):
        dq, dk, dv = [], [], []
        for h in range(2):
            cols = slice(h * HEAD, (h + 1) * HEAD)
            vcols = slice(BLK + h * HEAD, BLK + (h + 1) * HEAD)
            queries = q[layer, j * ROWS:(j + 1) * ROWS, cols]
            keys = kv[layer, j * ROWS:(j + 2) * ROWS, cols]
            values = kv[layer, j * ROWS:(j + 2) * ROWS, vcols]
            share = probs[layer, j, h]
            g = grad_out[:, cols]
            dp = nt(g, values)
            wide = share.astype(F32)
            r = jnp.sum(wide * dp, axis=-1, keepdims=True)
            ds = (wide * (dp - r) * SCALE).astype(BF)
            dq.append(nn(ds, keys))
            dk.append(tn(ds, queries))
            dv.append(tn(share, g))
        dqkv[j * ROWS:(j + 1) * ROWS, :BLK] = jnp.concatenate(dq, axis=1).astype(BF)
        return jnp.concatenate(dk + dv, axis=1)

    swap_r = [take("r", 2) for _ in range(LAYERS)]
    swap_sent = [batch(swap_send.at[layer]) for layer in range(LAYERS)]

    def project_back(layer, j):
        rows = slice(j * ROWS, (j + 1) * ROWS)
        lhs = dqkv[rows, :]
        for i in range(2):
            weight = w[layer, 2 * i + other].reshape(512, 3 * BLK)
            swap_send[layer, rows, i * 512:(i + 1) * 512] = nt(lhs, weight).astype(BF)
        src = swap_send.at[layer, pl.ds(j * ROWS, ROWS)]
        send(src, swap_recv.at[layer, pl.ds(j * ROWS, ROWS)], swap_r[layer] + j, partner, None, swap_sent[layer])
        for i in range(2):
            weight = w[layer, 2 * i + c].reshape(512, 3 * BLK)
            own[rows, i * 512:(i + 1) * 512] = nt(lhs, weight)

    def back_first(layer, grad):
        both = backward_segment(layer, 0, grad)
        halo_send[layer] = both[:ROWS].astype(BF)
        send(halo_send.at[layer], halo_recv.at[layer], halo_b[layer], group_dev(before))
        dkv[:ROWS, :] = both[ROWS:]

    def back_second(layer, grad):
        both = backward_segment(layer, 1, grad)
        dkv[ROWS:, :] = both[:ROWS]
        dkv_last[...] = both[ROWS:]

    rs1_r = take("r", 2)
    rs1_sent = batch(rs_send.at[1, :, pl.ds(0, 768)])
    rs0_r = take("r", 4)
    mine = pl.multiple_of(x * BLK, BLK)

    def swapped(layer, j):
        rows = slice(j * ROWS, (j + 1) * ROWS)
        arrive(swap_recv.at[layer, pl.ds(j * ROWS, ROWS)], swap_r[layer] + j)
        return own[rows, :] + swap_recv[layer, rows, :].astype(F32)

    def sum_one(j):
        rows = slice(j * ROWS, (j + 1) * ROWS)
        total = swapped(1, j)
        own[rows, :] = total
        rs_send[1, rows, :] = total.astype(BF)
        for k in range(3):
            col = pl.multiple_of(wrap(x + k + 1, 4) * BLK, BLK)
            src = rs_send.at[1, pl.ds(j * ROWS, ROWS), pl.ds(col, BLK)]
            send(src, rs1_recv.at[k, pl.ds(j * ROWS, ROWS)], rs1_r + j, peers[k], None, rs1_sent)
        g1[rows, :] = cotg[rows, :].astype(F32) + own[rows, pl.ds(mine, BLK)]

    def summed_one(j):
        rows = slice(j * ROWS, (j + 1) * ROWS)
        arrive(rs1_recv.at[:, pl.ds(j * ROWS, ROWS)], rs1_r + j)
        g1[rows, :] = (
            g1[rows, :] + rs1_recv[0, rows, :].astype(F32)
            + rs1_recv[1, rows, :].astype(F32) + rs1_recv[2, rows, :].astype(F32)
        )

    def sum_last(j):
        rows = slice(j * ROWS, (j + 1) * ROWS)
        own[rows, pl.ds(mine, BLK)] = own[rows, pl.ds(mine, BLK)] + g1[rows, :]
        rs_send[0, rows, :] = swapped(0, j).astype(BF)
        for half in range(2):
            src = rs_send.at[0, pl.ds(j * ROWS, ROWS), pl.ds(half * 512, 512)]
            here = (x == 2 * yl + j) & (yl == half)
            send(src, rs0_recv.at[x], rs0_r + x, dev(2 * yl + j, yh * 2 + half, z, c), jnp.logical_not(here))

            @pl.when(here)
            def _():
                rs0_recv[x] = rs_send[0, rows, half * 512:(half + 1) * 512]

    def back_own(layer):
        dqkv[:ROWS, BLK:] = (dkv[:ROWS, :] + dkv[ROWS:, :]).astype(BF)
        project_back(layer, 0)

    def back_halo(layer):
        arrive(halo_recv.at[layer], halo_b[layer])
        dqkv[ROWS:, BLK:] = (dkv_last[...] + halo_recv[layer].astype(F32)).astype(BF)
        project_back(layer, 1)

    for k in range(2):
        arrive(cotg.at[pl.ds(k * ROWS, ROWS)], a2a_c + k, away[k])
    last_states(0)
    back_first(1, cotg[:ROWS, :])
    last_states(1)
    back_second(1, cotg[ROWS:, :])
    back_own(1)
    sum_one(0)
    back_halo(1)
    sum_one(1)
    summed_one(0)
    back_first(0, g1[:ROWS, :].astype(BF))
    summed_one(1)
    back_second(0, g1[ROWS:, :].astype(BF))
    back_own(0)
    back_halo(0)
    sum_last(0)
    sum_last(1)

    for whole, index, cond in pending:
        copy = pltpu.make_async_remote_copy(
            src_ref=whole, dst_ref=whole, send_sem=ssem.at[index], recv_sem=rsem.at[0],
            device_id=partner, device_id_type=MESH,
        )
        when(cond, copy.wait_send)

    for k in range(2):
        arrive(outbuf.at[:, pl.ds(k * BLK, BLK)], out_r + k, away[k])
    out_ref[...] = outbuf[...]
    total = None
    for k in range(4):
        arrive(rs0_recv.at[k], rs0_r + k, jnp.logical_not(same & (x == k)))
    for k in range(4):
        term = rs0_recv[k].astype(F32)
        total = term if total is None else total + term
    grad_ref[...] = total

    assert counts["s"] <= N_SEND and counts["r"] <= N_RECV, counts


def per_device(inputs, cotangent, w_query, w_key, w_value, boundary):
    vmem = pl.BlockSpec(memory_space=pltpu.VMEM)
    scratch = [
        ((2, LAYERS, 16, 3 * BLK), BF),
        ((LAYERS, 4, 8, 2, 2, 16, 3 * BLK), BF),
        ((3 * ROWS, D), BF),
        ((3 * ROWS, D), BF),
        ((GROUP_ROWS, BLK), BF),
        ((LAYERS, 3 * ROWS, 2 * BLK), BF),
        ((LAYERS, GROUP_ROWS, BLK), BF),
        ((LAYERS, 2, 2, ROWS, GROUP_ROWS), BF),
        ((GROUP_ROWS, 2 * BLK), F32),
        ((ROWS, 2 * BLK), F32),
        ((LAYERS, ROWS, 2 * BLK), BF),
        ((LAYERS, ROWS, 2 * BLK), BF),
        ((GROUP_ROWS, 3 * BLK), BF),
        ((LAYERS, GROUP_ROWS, 1024), BF),
        ((LAYERS, GROUP_ROWS, 1024), BF),
        ((GROUP_ROWS, 1024), F32),
        ((LAYERS, GROUP_ROWS, 1024), BF),
        ((3, GROUP_ROWS, BLK), BF),
        ((4, ROWS, 512), BF),
        ((GROUP_ROWS, BLK), BF),
        ((ROWS, 512), BF),
        ((GROUP_ROWS, BLK), F32),
    ]
    return pl.pallas_call(
        kernel,
        out_shape=(
            jax.ShapeDtypeStruct((ROWS, 512), BF),
            jax.ShapeDtypeStruct((ROWS, 512), F32),
        ),
        in_specs=[pl.BlockSpec(memory_space=pl.ANY)] * 6,
        out_specs=(vmem, vmem),
        scratch_shapes=[pltpu.VMEM(shape, kind) for shape, kind in scratch]
        + [
            pltpu.VMEM((ROWS, 512), BF),
            pltpu.VMEM((ROWS, 512), BF),
            pltpu.SMEM((ROWS,), jnp.int32),
            pltpu.SemaphoreType.DMA((N_LOAD,)),
            pltpu.SemaphoreType.DMA((N_SEND,)), pltpu.SemaphoreType.DMA((N_RECV,)),
        ],
        compiler_params=pltpu.CompilerParams(
            collective_id=0, has_side_effects=True, vmem_limit_bytes=60 * 1024 * 1024
        ),
    )(inputs, cotangent, w_query, w_key, w_value, boundary)


def solution(mesh):
    return jax.shard_map(
        per_device,
        mesh=mesh,
        in_specs=(
            P("seg", "tp"),
            P("seg", "tp"),
            P(None, "seg", "tp"),
            P(None, "seg", "tp"),
            P(None, "seg", "tp"),
            P(),
        ),
        out_specs=(P("seg", "tp"), P("seg", "tp")),
        check_vma=False,
    )
```

```python
import math

import jax
import jax.numpy as jnp
from jax import lax
from jax.experimental import pallas as pl
from jax.experimental.pallas import tpu as pltpu
from jax.sharding import PartitionSpec as P

MESH = pl.DeviceIdType.MESH
HEAD = 128
LAYERS = 2
ROWS = 128
D = 2048
GROUP_ROWS = 2 * ROWS
BLK = 2 * HEAD
SCALE = 1.0 / math.sqrt(HEAD)
N_LOAD = 15
N_SEND = 36
N_RECV = 99
BF = jnp.bfloat16
F32 = jnp.float32


def nt(a, b):
    return lax.dot_general(a, b, (((1,), (1,)), ((), ())), preferred_element_type=F32)


def nn(a, b):
    return lax.dot_general(a, b, (((1,), (0,)), ((), ())), preferred_element_type=F32)


def tn(a, b):
    return lax.dot_general(a, b, (((0,), (0,)), ((), ())), preferred_element_type=F32)


def kernel(
    x_hbm, cot_hbm, wq, wk, wv, bound_hbm,
    out_ref, grad_ref,
    stage, w, x0, x1, cotg, kv, q, probs, dkv, dkv_last, halo_send, halo_recv, dqkv,
    swap_send, swap_recv, own, rs_send, rs1_recv, rs0_recv, x2, outbuf, g1,
    x_in, cot_in, bound, lsem, ssem, rsem,
):
    seg = lax.axis_index("seg")
    tp = lax.axis_index("tp")
    x = lax.rem(seg, 4)
    z = lax.rem(lax.div(seg, 4), 8)
    yh = lax.div(seg, 32)
    yl = lax.div(tp, 2)
    c = lax.rem(tp, 2)
    y = yh * 2 + yl
    other = 1 - c
    xh = lax.div(x, 2)
    xl = lax.rem(x, 2)

    def dev(dx, dy, dz, dc):
        return (lax.div(dy, 2) * 32 + dz * 4 + dx, lax.rem(dy, 2) * 2 + dc)

    def wrap(value, n):
        return lax.rem(value + n, n)

    me_y = y
    pair_y = yh * 2 + (1 - yl)
    group = yh * 16 + z * 2 + yl
    after = wrap(group + 1, 64)
    before = wrap(group - 1, 64)

    def group_dev(g):
        gy = lax.div(g, 16) * 2 + lax.rem(g, 2)
        return dev(x, gy, lax.rem(lax.div(g, 2), 8), c)

    partner = dev(x, y, z, other)
    peers = [dev(wrap(x + k, 4), y, z, c) for k in (1, 2, 3)]

    counts = {"s": 0, "r": 0}
    pending = []

    def take(kind, n=1):
        first = counts[kind]
        counts[kind] += n
        return first

    def batch(whole, cond=None):
        index = take("s")
        pending.append((whole, index, cond))
        return index

    def when(cond, action):
        if cond is None:
            action()
        else:
            pl.when(cond)(action)

    def send(src, dst, recv, target, cond=None, index=None):
        copy = pltpu.make_async_remote_copy(
            src_ref=src, dst_ref=dst, send_sem=ssem.at[batch(src, cond) if index is None else index],
            recv_sem=rsem.at[recv], device_id=target, device_id_type=MESH,
        )
        when(cond, copy.start)

    def arrive(dst, recv, cond=None):
        copy = pltpu.make_async_remote_copy(
            src_ref=dst, dst_ref=dst, send_sem=ssem.at[0], recv_sem=rsem.at[recv],
            device_id=partner, device_id_type=MESH,
        )
        when(cond, copy.wait_recv)

    loads = []

    def load(src, dst):
        copy = pltpu.make_async_copy(src, dst, lsem.at[len(loads)])
        copy.start()
        loads.append(copy)

    for layer in range(LAYERS):
        for j in range(2):
            for t, ref in enumerate((wq, wk, wv)):
                load(ref.at[layer, :, pl.ds(j * BLK, BLK)], stage.at[j, layer, :, pl.ds(t * BLK, BLK)])
    load(x_hbm, x_in)
    load(cot_hbm, cot_in)
    load(bound_hbm, bound)

    barrier = pltpu.get_barrier_semaphore()
    known = list(peers) + [partner, group_dev(after), group_dev(before)]
    known += [dev(wrap(x + k, 4), pair_y, z, c) for k in (1, 2, 3)]
    known += [dev(x, y, wrap(z + k, 8), c) for k in range(1, 8)]
    known += [dev(x, wrap(y + k, 8), z, c) for k in range(1, 8)]
    for device in known:
        pl.semaphore_signal(barrier, inc=1, device_id=device, device_id_type=MESH)
    for copy in loads:
        copy.wait()
    pl.semaphore_wait(barrier, len(known))

    same = xh == yl
    home = [same & (xl == j) for j in range(2)]
    away = [jnp.logical_not(h) for h in home]
    dest_y = yh * 2 + xh
    own_col = pl.multiple_of(xh * 1024 + c * 512 + xl * BLK, BLK)

    a2a_w = [take("r", 2) for _ in range(LAYERS)]
    a2a_c = take("r", 2)

    def spread_weights(layer):
        for j in range(2):
            dst = w.at[layer, yh, z, xh, xl]
            send(stage.at[j, layer], dst, a2a_w[layer] + xl, dev(2 * yl + j, dest_y, z, c), away[j])

            @pl.when(home[j])
            def _():
                w[layer, yh, z, xh, xl] = stage[j, layer]

    def spread_weights_wait(layer):
        for k in range(2):
            arrive(w.at[layer, yh, z, yl, k], a2a_w[layer] + k, away[k])

    spread_weights(0)
    spread_weights(1)

    x0_x = [[take("r") for _ in range(2)] for _ in range(2)]
    x0_c = take("r")
    x0_ring = batch(x0.at[pl.ds(0, GROUP_ROWS), pl.ds(0, 1536)], same)
    x0_pair = batch(x0.at[pl.ds(0, GROUP_ROWS), pl.ds(0, 1024)])
    last_r, last_x, last_c = take("r", LAYERS), take("r", LAYERS), take("r", LAYERS)
    last_sent = [batch(x0.at[pl.ds(0, GROUP_ROWS), pl.ds(0, 1024)]) for _ in range(LAYERS)]
    states_of = (x0, x1)
    my_rows = pl.multiple_of(xl * ROWS, ROWS)
    my_cols = pl.multiple_of(tp * 512, 512)

    @pl.when(same)
    def _():
        x0[pl.ds(ROWS + my_rows, ROWS), pl.ds(my_cols, 512)] = x_in[...]

    send(
        x_in, x0.at[pl.ds(ROWS + my_rows, ROWS), pl.ds(my_cols, 512)], x0_x[0][0] + xl * 2 + yl,
        dev(x, pair_y, z, c), jnp.logical_not(same),
    )

    def x0_piece(j, half, core):
        return x0.at[pl.ds((j + 1) * ROWS, ROWS), pl.ds(pl.multiple_of(half * 1024 + core * 512, 512), 512)]

    def x0_ring_send(j, half, local):
        piece = x0_piece(j, half, c)
        cond = home[j] & ((yl == half) if local else (yl != half))
        if not local:
            arrive(piece, x0_x[j][half], cond)
        for target in peers:
            send(piece, piece, x0_x[j][half], target, cond, x0_ring)

    def x0_swap(j, half):
        piece = x0_piece(j, half, c)
        arrive(piece, x0_x[j][half], away[j])
        send(piece, piece, x0_c, partner, None, x0_pair)

    def x0_all(action, *rest):
        for j in range(2):
            for half in range(2):
                action(j, half, *rest)

    x0_all(x0_ring_send, True)

    def quarter(layer, row, xs, core):
        col = lax.div(xs, 2) * 1024 + core * 512 + lax.rem(xs, 2) * BLK
        return states_of[layer].at[pl.ds(row, ROWS), pl.ds(pl.multiple_of(col, BLK), BLK)]

    def last_send(layer):
        piece, dst = quarter(layer, 2 * ROWS, x, c), quarter(layer, 0, x, c)
        send(piece, dst, last_r + layer, group_dev(after), None, last_sent[layer])

    def last_spread(layer):
        piece = quarter(layer, 0, x, c)
        arrive(piece, last_r + layer)
        for target in peers:
            send(piece, piece, last_x + layer, target, None, last_sent[layer])
        send(piece, piece, last_c + layer, partner, None, last_sent[layer])

    def last_swap(layer):
        arrive(states_of[layer].at[pl.ds(0, ROWS), pl.ds(0, 768)], last_x + layer)
        for k in range(3):
            piece = quarter(layer, 0, wrap(x - k - 1, 4), c)
            send(piece, piece, last_c + layer, partner, None, last_sent[layer])

    def last_wait(layer):
        arrive(states_of[layer].at[pl.ds(0, ROWS), pl.ds(0, 1024)], last_c + layer)

    def spread_cotangent():
        for j in range(2):
            dst = cotg.at[pl.ds(my_rows, ROWS)]
            src = cot_in.at[:, pl.ds(j * BLK, BLK)]
            send(src, dst, a2a_c + xl, dev(2 * yl + j, dest_y, z, c), away[j])

            @pl.when(home[j])
            def _():
                cotg[pl.ds(my_rows, ROWS)] = cot_in[:, j * BLK:(j + 1) * BLK]

    out_z = 2 * lax.rem(z, 2) - 1
    out_y = 2 * yl - 1
    one = {(kind, rel): take("r") for kind in range(2) for rel in range(4)}
    direct = take("r", 2)

    def farthest(s, right):
        return 4 if (s == 0) == right else 3

    two = {
        (layer, kind, s, right, d): take("r")
        for layer in range(LAYERS) for kind in range(2) for s in range(2) for right in (False, True)
        for d in range(1, 4)
    }
    two_end = take("r", LAYERS)

    next_to = [
        {k: dev(x, y, wrap(z + k, 8), c) for k in (1, -1)},
        {k: dev(x, wrap(y + k, 8), z, c) for k in (1, -1)},
    ]
    outer = [dev(x, y, wrap(z + out_z, 8), c), dev(x, wrap(y + out_y, 8), z, c)]
    mate = [dev(x, y, z - out_z, c), dev(x, y - out_y, z, c)]
    z_at = {k: wrap(z + k, 8) for k in range(-4, 5)}
    y_at = {k: (lax.div(wrap(y + k, 8), 2), lax.rem(wrap(y + k, 8), 2)) for k in range(-4, 5)}
    z_pair = lax.div(z, 2)
    pairs = [
        [z_pair * 2] + [wrap(z_pair + k, 4) * 2 for k in (out_z, -out_z, 2)],
        [yh] + [wrap(yh + k, 4) for k in (out_y, -out_y, 2)],
    ]

    def block(layer, kind, at_mate):
        if kind == 0:
            return w.at[layer, yh, z - out_z if at_mate else z, yl, 0]
        return w.at[layer, yh, z, 1 - yl if at_mate else yl, 1]

    def pair(layer, kind, rel, shift):
        if kind == 0:
            at = y_at[shift]
            return w.at[layer, at[0], pl.ds(pairs[0][rel], 2), at[1], 0]
        return w.at[layer, pairs[1][rel], z_at[shift], :, 1]

    def part(layer, kind, s, shift):
        if kind == 0:
            return w.at[layer, y_at[shift][0], pl.ds(4 * s, 4), y_at[shift][1], 0]
        return w.at[layer, pl.ds(2 * s, 2), z_at[shift], :, 1]

    batch_one = [[batch(w.at[layer, 0, pl.ds(0, 7), 0, 0]) for _ in range(2)] for layer in range(LAYERS)]
    batch_two = {
        (layer, kind, s): batch(w.at[layer, :, pl.ds(0, 6 if layer + kind + s == 0 else 7), 0, 0])
        for layer in range(LAYERS) for kind in range(2) for s in range(2)
    }
    lead = take("s")

    def pass_on(layer, kind, s, right, d):
        if d < farthest(s, right):
            piece = part(layer, kind, s, 0 if d == 0 else (-d if right else d))
            index = lead if right and layer + kind + s + d == 0 else batch_two[layer, kind, s]
            recv = two[layer, kind, s, right, d + 1] if d < 3 else two_end + layer
            send(piece, piece, recv, next_to[1 - kind][1 if right else -1], None, index)

    def ring(layer, s, d):
        for kind in range(2):
            for right in (False, True):
                if 1 <= d <= 3:
                    arrive(part(layer, kind, s, -d if right else d), two[layer, kind, s, right, d])
                pass_on(layer, kind, s, right, d)

    def ring_end(layer):
        arrive(w.at[layer, 0, :, :, 0], two_end + layer)

    def direct_send():
        for k in (1, -1, 2, -2, 3, -3, 4):
            for kind in range(2):
                mine = block(0, kind, False)
                to = wrap((z if kind == 0 else y) + k, 8)
                target = dev(x, y, to, c) if kind == 0 else dev(x, to, z, c)
                send(mine, mine, direct + kind, target, None, batch_one[0][kind])

    def direct_wait():
        for kind in range(2):
            arrive(w.at[0, 0, pl.ds(0, 7), 0, kind], direct + kind)

    def relay(t):
        for kind in range(2):
            if t == 0:
                mine = block(1, kind, False)
                send(mine, mine, one[kind, 0], mate[kind], None, batch_one[1][kind])
                continue
            rel = t - 1
            if rel == 0:
                arrive(block(1, kind, True), one[kind, 0])
            else:
                arrive(pair(1, kind, rel, 0), one[kind, rel])
            if rel < 3:
                piece = pair(1, kind, rel, 0)
                send(piece, piece, one[kind, rel + 1], (mate if rel == 1 else outer)[kind], None, batch_one[1][kind])

    spread_weights_wait(0)
    direct_send()
    spread_weights_wait(1)
    relay(0)
    direct_wait()
    ring(0, 0, 0)
    x0_all(x0_ring_send, False)
    relay(1)
    head = part(0, 0, 0, 0)
    pltpu.make_async_remote_copy(
        src_ref=head, dst_ref=head, send_sem=ssem.at[lead], recv_sem=rsem.at[0],
        device_id=partner, device_id_type=MESH,
    ).wait_send()
    ring(0, 1, 0)
    ring(0, 0, 1)
    relay(2)
    x0_all(x0_swap)
    last_send(0)
    ring(0, 1, 1)
    relay(3)
    ring(0, 0, 2)
    relay(4)
    ring(0, 1, 2)
    last_spread(0)
    ring(0, 0, 3)
    ring(1, 0, 0)
    ring(0, 1, 3)
    ring(1, 1, 0)
    last_swap(0)
    spread_cotangent()
    ring_end(0)
    arrive(x0.at[pl.ds(0, GROUP_ROWS), pl.ds(0, 1024)], x0_c)
    last_wait(0)

    pos_q = lax.broadcasted_iota(jnp.int32, (ROWS, GROUP_ROWS), 0)
    pos_k = lax.broadcasted_iota(jnp.int32, (ROWS, GROUP_ROWS), 1)

    def mask(j):
        s = 2 * group + j
        now = bound[s]
        prev = bound[jnp.maximum(s - 1, 0)]
        first = jnp.where(prev == ROWS, 0, prev)
        first = jnp.where(s > 0, first, ROWS)
        pos_m = pos_k - ROWS
        memory = (pos_k < ROWS) & (pos_q < now) & (pos_k >= first)
        segment = (pos_m >= 0) & (pos_m <= pos_q) & ((pos_m >= now) | (pos_q < now))
        return memory | segment

    halo_b = [take("r") for _ in range(LAYERS)]

    def project(layer, states):
        def columns(first, last):
            total = None
            for part in range(4):
                weight = w[layer, part].reshape(512, 3 * BLK)[:, first:last]
                rows = slice(0 if first else ROWS, None)
                term = nn(states[rows, part * 512:(part + 1) * 512], weight)
                total = term if total is None else total + term
            return total.astype(BF)

        kv[layer] = columns(BLK, 3 * BLK)
        q[layer] = columns(0, BLK)

    def attend(layer, j):
        visible = mask(j)
        results = []
        for h in range(2):
            cols = slice(h * HEAD, (h + 1) * HEAD)
            vcols = slice(BLK + h * HEAD, BLK + (h + 1) * HEAD)
            queries = q[layer, j * ROWS:(j + 1) * ROWS, cols]
            keys = kv[layer, j * ROWS:(j + 2) * ROWS, cols]
            values = kv[layer, j * ROWS:(j + 2) * ROWS, vcols]
            scores = jnp.where(visible, nt(queries, keys) * SCALE, -1e30)
            raised = jnp.exp(scores - jnp.max(scores, axis=-1, keepdims=True))
            share = (raised / jnp.sum(raised, axis=-1, keepdims=True)).astype(BF)
            probs[layer, j, h] = share
            results.append(nn(share, values))
        return jnp.concatenate(results, axis=1)

    def x1_piece(j, xs, core):
        return quarter(1, (j + 1) * ROWS, xs, core)

    x1_x = [take("r", 3) for _ in range(2)]
    x1_c = take("r", 2)
    x1_sent = batch(x1.at[pl.ds(0, GROUP_ROWS), pl.ds(0, 1792)])

    def step_states(j):
        before_states = x0[(j + 1) * ROWS:(j + 2) * ROWS, pl.ds(own_col, BLK)]
        x1[(j + 1) * ROWS:(j + 2) * ROWS, pl.ds(own_col, BLK)] = (
            before_states.astype(F32) + attend(0, j)
        ).astype(BF)
        piece = x1_piece(j, x, c)
        for k in range(3):
            send(piece, piece, x1_x[j] + k, peers[k], None, x1_sent)
        send(piece, piece, x1_c + j, partner, None, x1_sent)

    def gather_states(j):
        for k in range(3):
            piece = x1_piece(j, wrap(x - k - 1, 4), c)
            arrive(piece, x1_x[j] + k)
            send(piece, piece, x1_c + j, partner, None, x1_sent)

    def gather_states_wait(j):
        arrive(x1.at[pl.ds((j + 1) * ROWS, ROWS), pl.ds(0, 1024)], x1_c + j)

    project(0, x0)
    ring(1, 0, 1)
    step_states(1)
    last_send(1)
    ring(1, 1, 1)
    step_states(0)
    ring(1, 0, 2)
    gather_states(1)
    ring(1, 1, 2)
    last_spread(1)
    gather_states(0)
    ring(1, 0, 3)
    ring(1, 1, 3)
    last_swap(1)
    gather_states_wait(1)
    gather_states_wait(0)
    ring_end(1)
    last_wait(1)
    project(1, x1)

    out_r = take("r", 2)

    def last_states(j):
        before_states = x1[(j + 1) * ROWS:(j + 2) * ROWS, pl.ds(own_col, BLK)]
        x2[j * ROWS:(j + 1) * ROWS, :] = (before_states.astype(F32) + attend(1, j)).astype(BF)
        dst = outbuf.at[:, pl.ds(pl.multiple_of(xl * BLK, BLK), BLK)]
        src = x2.at[pl.ds(j * ROWS, ROWS)]
        send(src, dst, out_r + xl, dev(2 * yl + j, dest_y, z, c), away[j])

        @pl.when(home[j])
        def _():
            outbuf[:, pl.ds(pl.multiple_of(xl * BLK, BLK), BLK)] = x2[j * ROWS:(j + 1) * ROWS, :]

    def backward_segment(layer, j, grad_out):
        dq, dk, dv = [], [], []
        for h in range(2):
            cols = slice(h * HEAD, (h + 1) * HEAD)
            vcols = slice(BLK + h * HEAD, BLK + (h + 1) * HEAD)
            queries = q[layer, j * ROWS:(j + 1) * ROWS, cols]
            keys = kv[layer, j * ROWS:(j + 2) * ROWS, cols]
            values = kv[layer, j * ROWS:(j + 2) * ROWS, vcols]
            share = probs[layer, j, h]
            g = grad_out[:, cols]
            dp = nt(g, values)
            wide = share.astype(F32)
            r = jnp.sum(wide * dp, axis=-1, keepdims=True)
            ds = (wide * (dp - r) * SCALE).astype(BF)
            dq.append(nn(ds, keys))
            dk.append(tn(ds, queries))
            dv.append(tn(share, g))
        dqkv[j * ROWS:(j + 1) * ROWS, :BLK] = jnp.concatenate(dq, axis=1).astype(BF)
        return jnp.concatenate(dk + dv, axis=1)

    swap_r = [take("r", 2) for _ in range(LAYERS)]
    swap_sent = [batch(swap_send.at[layer]) for layer in range(LAYERS)]

    def project_back(layer, j):
        rows = slice(j * ROWS, (j + 1) * ROWS)
        lhs = dqkv[rows, :]
        for i in range(2):
            weight = w[layer, 2 * i + other].reshape(512, 3 * BLK)
            swap_send[layer, rows, i * 512:(i + 1) * 512] = nt(lhs, weight).astype(BF)
        src = swap_send.at[layer, pl.ds(j * ROWS, ROWS)]
        send(src, swap_recv.at[layer, pl.ds(j * ROWS, ROWS)], swap_r[layer] + j, partner, None, swap_sent[layer])
        for i in range(2):
            weight = w[layer, 2 * i + c].reshape(512, 3 * BLK)
            own[rows, i * 512:(i + 1) * 512] = nt(lhs, weight)

    def back_first(layer, grad):
        both = backward_segment(layer, 0, grad)
        halo_send[layer] = both[:ROWS].astype(BF)
        send(halo_send.at[layer], halo_recv.at[layer], halo_b[layer], group_dev(before))
        dkv[:ROWS, :] = both[ROWS:]

    def back_second(layer, grad):
        both = backward_segment(layer, 1, grad)
        dkv[ROWS:, :] = both[:ROWS]
        dkv_last[...] = both[ROWS:]

    rs1_r = take("r", 2)
    rs1_sent = batch(rs_send.at[1, :, pl.ds(0, 768)])
    rs0_r = take("r", 4)
    mine = pl.multiple_of(x * BLK, BLK)

    def swapped(layer, j):
        rows = slice(j * ROWS, (j + 1) * ROWS)
        arrive(swap_recv.at[layer, pl.ds(j * ROWS, ROWS)], swap_r[layer] + j)
        return own[rows, :] + swap_recv[layer, rows, :].astype(F32)

    def sum_one(j):
        rows = slice(j * ROWS, (j + 1) * ROWS)
        total = swapped(1, j)
        own[rows, :] = total
        rs_send[1, rows, :] = total.astype(BF)
        for k in range(3):
            col = pl.multiple_of(wrap(x + k + 1, 4) * BLK, BLK)
            src = rs_send.at[1, pl.ds(j * ROWS, ROWS), pl.ds(col, BLK)]
            send(src, rs1_recv.at[k, pl.ds(j * ROWS, ROWS)], rs1_r + j, peers[k], None, rs1_sent)
        g1[rows, :] = cotg[rows, :].astype(F32) + own[rows, pl.ds(mine, BLK)]

    def summed_one(j):
        rows = slice(j * ROWS, (j + 1) * ROWS)
        arrive(rs1_recv.at[:, pl.ds(j * ROWS, ROWS)], rs1_r + j)
        g1[rows, :] = (
            g1[rows, :] + rs1_recv[0, rows, :].astype(F32)
            + rs1_recv[1, rows, :].astype(F32) + rs1_recv[2, rows, :].astype(F32)
        )

    def sum_last(j):
        rows = slice(j * ROWS, (j + 1) * ROWS)
        own[rows, pl.ds(mine, BLK)] = own[rows, pl.ds(mine, BLK)] + g1[rows, :]
        rs_send[0, rows, :] = swapped(0, j).astype(BF)
        for half in range(2):
            src = rs_send.at[0, pl.ds(j * ROWS, ROWS), pl.ds(half * 512, 512)]
            here = (x == 2 * yl + j) & (yl == half)
            send(src, rs0_recv.at[x], rs0_r + x, dev(2 * yl + j, yh * 2 + half, z, c), jnp.logical_not(here))

            @pl.when(here)
            def _():
                rs0_recv[x] = rs_send[0, rows, half * 512:(half + 1) * 512]

    def back_own(layer):
        dqkv[:ROWS, BLK:] = (dkv[:ROWS, :] + dkv[ROWS:, :]).astype(BF)
        project_back(layer, 0)

    def back_halo(layer):
        arrive(halo_recv.at[layer], halo_b[layer])
        dqkv[ROWS:, BLK:] = (dkv_last[...] + halo_recv[layer].astype(F32)).astype(BF)
        project_back(layer, 1)

    for k in range(2):
        arrive(cotg.at[pl.ds(k * ROWS, ROWS)], a2a_c + k, away[k])
    last_states(0)
    back_first(1, cotg[:ROWS, :])
    last_states(1)
    back_second(1, cotg[ROWS:, :])
    back_own(1)
    sum_one(0)
    back_halo(1)
    sum_one(1)
    summed_one(0)
    back_first(0, g1[:ROWS, :].astype(BF))
    summed_one(1)
    back_second(0, g1[ROWS:, :].astype(BF))
    back_own(0)
    sum_last(0)
    back_halo(0)
    sum_last(1)

    for whole, index, cond in pending:
        copy = pltpu.make_async_remote_copy(
            src_ref=whole, dst_ref=whole, send_sem=ssem.at[index], recv_sem=rsem.at[0],
            device_id=partner, device_id_type=MESH,
        )
        when(cond, copy.wait_send)

    for k in range(2):
        arrive(outbuf.at[:, pl.ds(k * BLK, BLK)], out_r + k, away[k])
    out_ref[...] = outbuf[...]
    total = None
    for k in range(4):
        arrive(rs0_recv.at[k], rs0_r + k, jnp.logical_not(same & (x == k)))
    for k in range(4):
        term = rs0_recv[k].astype(F32)
        total = term if total is None else total + term
    grad_ref[...] = total

    assert counts["s"] <= N_SEND and counts["r"] <= N_RECV, counts


def per_device(inputs, cotangent, w_query, w_key, w_value, boundary):
    vmem = pl.BlockSpec(memory_space=pltpu.VMEM)
    scratch = [
        ((2, LAYERS, 16, 3 * BLK), BF),
        ((LAYERS, 4, 8, 2, 2, 16, 3 * BLK), BF),
        ((3 * ROWS, D), BF),
        ((3 * ROWS, D), BF),
        ((GROUP_ROWS, BLK), BF),
        ((LAYERS, 3 * ROWS, 2 * BLK), BF),
        ((LAYERS, GROUP_ROWS, BLK), BF),
        ((LAYERS, 2, 2, ROWS, GROUP_ROWS), BF),
        ((GROUP_ROWS, 2 * BLK), F32),
        ((ROWS, 2 * BLK), F32),
        ((LAYERS, ROWS, 2 * BLK), BF),
        ((LAYERS, ROWS, 2 * BLK), BF),
        ((GROUP_ROWS, 3 * BLK), BF),
        ((LAYERS, GROUP_ROWS, 1024), BF),
        ((LAYERS, GROUP_ROWS, 1024), BF),
        ((GROUP_ROWS, 1024), F32),
        ((LAYERS, GROUP_ROWS, 1024), BF),
        ((3, GROUP_ROWS, BLK), BF),
        ((4, ROWS, 512), BF),
        ((GROUP_ROWS, BLK), BF),
        ((ROWS, 512), BF),
        ((GROUP_ROWS, BLK), F32),
    ]
    return pl.pallas_call(
        kernel,
        out_shape=(
            jax.ShapeDtypeStruct((ROWS, 512), BF),
            jax.ShapeDtypeStruct((ROWS, 512), F32),
        ),
        in_specs=[pl.BlockSpec(memory_space=pl.ANY)] * 6,
        out_specs=(vmem, vmem),
        scratch_shapes=[pltpu.VMEM(shape, kind) for shape, kind in scratch]
        + [
            pltpu.VMEM((ROWS, 512), BF),
            pltpu.VMEM((ROWS, 512), BF),
            pltpu.SMEM((ROWS,), jnp.int32),
            pltpu.SemaphoreType.DMA((N_LOAD,)),
            pltpu.SemaphoreType.DMA((N_SEND,)), pltpu.SemaphoreType.DMA((N_RECV,)),
        ],
        compiler_params=pltpu.CompilerParams(
            collective_id=0, has_side_effects=True, vmem_limit_bytes=60 * 1024 * 1024
        ),
    )(inputs, cotangent, w_query, w_key, w_value, boundary)


def solution(mesh):
    return jax.shard_map(
        per_device,
        mesh=mesh,
        in_specs=(
            P("seg", "tp"),
            P("seg", "tp"),
            P(None, "seg", "tp"),
            P(None, "seg", "tp"),
            P(None, "seg", "tp"),
            P(),
        ),
        out_specs=(P("seg", "tp"), P("seg", "tp")),
        check_vma=False,
    )
```

```python
import math

import jax
import jax.numpy as jnp
from jax import lax
from jax.experimental import pallas as pl
from jax.experimental.pallas import tpu as pltpu
from jax.sharding import PartitionSpec as P

MESH = pl.DeviceIdType.MESH
HEAD = 128
LAYERS = 2
ROWS = 128
D = 2048
GROUP_ROWS = 2 * ROWS
BLK = 2 * HEAD
SCALE = 1.0 / math.sqrt(HEAD)
N_LOAD = 15
N_SEND = 36
N_RECV = 99
BF = jnp.bfloat16
F32 = jnp.float32


def nt(a, b):
    return lax.dot_general(a, b, (((1,), (1,)), ((), ())), preferred_element_type=F32)


def nn(a, b):
    return lax.dot_general(a, b, (((1,), (0,)), ((), ())), preferred_element_type=F32)


def tn(a, b):
    return lax.dot_general(a, b, (((0,), (0,)), ((), ())), preferred_element_type=F32)


def kernel(
    x_hbm, cot_hbm, wq, wk, wv, bound_hbm,
    out_ref, grad_ref,
    stage, w, x0, x1, cotg, kv, q, probs, dkv, dkv_last, halo_send, halo_recv, dqkv,
    swap_send, swap_recv, own, rs_send, rs1_recv, rs0_recv, x2, outbuf, g1,
    x_in, cot_in, bound, lsem, ssem, rsem,
):
    seg = lax.axis_index("seg")
    tp = lax.axis_index("tp")
    x = lax.rem(seg, 4)
    z = lax.rem(lax.div(seg, 4), 8)
    yh = lax.div(seg, 32)
    yl = lax.div(tp, 2)
    c = lax.rem(tp, 2)
    y = yh * 2 + yl
    other = 1 - c
    xh = lax.div(x, 2)
    xl = lax.rem(x, 2)

    def dev(dx, dy, dz, dc):
        return (lax.div(dy, 2) * 32 + dz * 4 + dx, lax.rem(dy, 2) * 2 + dc)

    def wrap(value, n):
        return lax.rem(value + n, n)

    me_y = y
    pair_y = yh * 2 + (1 - yl)
    group = yh * 16 + z * 2 + yl
    after = wrap(group + 1, 64)
    before = wrap(group - 1, 64)

    def group_dev(g):
        gy = lax.div(g, 16) * 2 + lax.rem(g, 2)
        return dev(x, gy, lax.rem(lax.div(g, 2), 8), c)

    partner = dev(x, y, z, other)
    peers = [dev(wrap(x + k, 4), y, z, c) for k in (1, 2, 3)]

    counts = {"s": 0, "r": 0}
    pending = []

    def take(kind, n=1):
        first = counts[kind]
        counts[kind] += n
        return first

    def batch(whole, cond=None):
        index = take("s")
        pending.append((whole, index, cond))
        return index

    def when(cond, action):
        if cond is None:
            action()
        else:
            pl.when(cond)(action)

    def send(src, dst, recv, target, cond=None, index=None):
        copy = pltpu.make_async_remote_copy(
            src_ref=src, dst_ref=dst, send_sem=ssem.at[batch(src, cond) if index is None else index],
            recv_sem=rsem.at[recv], device_id=target, device_id_type=MESH,
        )
        when(cond, copy.start)

    def arrive(dst, recv, cond=None):
        copy = pltpu.make_async_remote_copy(
            src_ref=dst, dst_ref=dst, send_sem=ssem.at[0], recv_sem=rsem.at[recv],
            device_id=partner, device_id_type=MESH,
        )
        when(cond, copy.wait_recv)

    loads = []

    def load(src, dst):
        copy = pltpu.make_async_copy(src, dst, lsem.at[len(loads)])
        copy.start()
        loads.append(copy)

    for layer in range(LAYERS):
        for j in range(2):
            for t, ref in enumerate((wq, wk, wv)):
                load(ref.at[layer, :, pl.ds(j * BLK, BLK)], stage.at[j, layer, :, pl.ds(t * BLK, BLK)])
    load(x_hbm, x_in)
    load(cot_hbm, cot_in)
    load(bound_hbm, bound)

    barrier = pltpu.get_barrier_semaphore()
    known = list(peers) + [partner, group_dev(after), group_dev(before)]
    known += [dev(wrap(x + k, 4), pair_y, z, c) for k in (1, 2, 3)]
    known += [dev(x, y, wrap(z + k, 8), c) for k in range(1, 8)]
    known += [dev(x, wrap(y + k, 8), z, c) for k in range(1, 8)]
    for device in known:
        pl.semaphore_signal(barrier, inc=1, device_id=device, device_id_type=MESH)
    for copy in loads:
        copy.wait()
    pl.semaphore_wait(barrier, len(known))

    same = xh == yl
    home = [same & (xl == j) for j in range(2)]
    away = [jnp.logical_not(h) for h in home]
    dest_y = yh * 2 + xh
    own_col = pl.multiple_of(xh * 1024 + c * 512 + xl * BLK, BLK)

    a2a_w = [take("r", 2) for _ in range(LAYERS)]
    a2a_c = take("r", 2)

    def spread_weights(layer):
        for j in range(2):
            dst = w.at[layer, yh, z, xh, xl]
            send(stage.at[j, layer], dst, a2a_w[layer] + xl, dev(2 * yl + j, dest_y, z, c), away[j])

            @pl.when(home[j])
            def _():
                w[layer, yh, z, xh, xl] = stage[j, layer]

    def spread_weights_wait(layer):
        for k in range(2):
            arrive(w.at[layer, yh, z, yl, k], a2a_w[layer] + k, away[k])

    spread_weights(0)
    spread_weights(1)

    x0_x = [[take("r") for _ in range(2)] for _ in range(2)]
    x0_c = take("r")
    x0_ring = batch(x0.at[pl.ds(0, GROUP_ROWS), pl.ds(0, 1536)], same)
    x0_pair = batch(x0.at[pl.ds(0, GROUP_ROWS), pl.ds(0, 1024)])
    last_r, last_x, last_c = take("r", LAYERS), take("r", LAYERS), take("r", LAYERS)
    last_sent = [batch(x0.at[pl.ds(0, GROUP_ROWS), pl.ds(0, 1024)]) for _ in range(LAYERS)]
    states_of = (x0, x1)
    my_rows = pl.multiple_of(xl * ROWS, ROWS)
    my_cols = pl.multiple_of(tp * 512, 512)

    @pl.when(same)
    def _():
        x0[pl.ds(ROWS + my_rows, ROWS), pl.ds(my_cols, 512)] = x_in[...]

    send(
        x_in, x0.at[pl.ds(ROWS + my_rows, ROWS), pl.ds(my_cols, 512)], x0_x[0][0] + xl * 2 + yl,
        dev(x, pair_y, z, c), jnp.logical_not(same),
    )

    def x0_piece(j, half, core):
        return x0.at[pl.ds((j + 1) * ROWS, ROWS), pl.ds(pl.multiple_of(half * 1024 + core * 512, 512), 512)]

    def x0_ring_send(j, half, local):
        piece = x0_piece(j, half, c)
        cond = home[j] & ((yl == half) if local else (yl != half))
        if not local:
            arrive(piece, x0_x[j][half], cond)
        for target in peers:
            send(piece, piece, x0_x[j][half], target, cond, x0_ring)

    def x0_swap(j, half):
        piece = x0_piece(j, half, c)
        arrive(piece, x0_x[j][half], away[j])
        send(piece, piece, x0_c, partner, None, x0_pair)

    def x0_all(action, *rest):
        for j in range(2):
            for half in range(2):
                action(j, half, *rest)

    x0_all(x0_ring_send, True)

    def quarter(layer, row, xs, core):
        col = lax.div(xs, 2) * 1024 + core * 512 + lax.rem(xs, 2) * BLK
        return states_of[layer].at[pl.ds(row, ROWS), pl.ds(pl.multiple_of(col, BLK), BLK)]

    def last_send(layer):
        piece, dst = quarter(layer, 2 * ROWS, x, c), quarter(layer, 0, x, c)
        send(piece, dst, last_r + layer, group_dev(after), None, last_sent[layer])

    def last_spread(layer):
        piece = quarter(layer, 0, x, c)
        arrive(piece, last_r + layer)
        for target in peers:
            send(piece, piece, last_x + layer, target, None, last_sent[layer])
        send(piece, piece, last_c + layer, partner, None, last_sent[layer])

    def last_swap(layer):
        arrive(states_of[layer].at[pl.ds(0, ROWS), pl.ds(0, 768)], last_x + layer)
        for k in range(3):
            piece = quarter(layer, 0, wrap(x - k - 1, 4), c)
            send(piece, piece, last_c + layer, partner, None, last_sent[layer])

    def last_wait(layer):
        arrive(states_of[layer].at[pl.ds(0, ROWS), pl.ds(0, 1024)], last_c + layer)

    def spread_cotangent():
        for j in range(2):
            dst = cotg.at[pl.ds(my_rows, ROWS)]
            src = cot_in.at[:, pl.ds(j * BLK, BLK)]
            send(src, dst, a2a_c + xl, dev(2 * yl + j, dest_y, z, c), away[j])

            @pl.when(home[j])
            def _():
                cotg[pl.ds(my_rows, ROWS)] = cot_in[:, j * BLK:(j + 1) * BLK]

    out_z = 2 * lax.rem(z, 2) - 1
    out_y = 2 * yl - 1
    one = {(kind, rel): take("r") for kind in range(2) for rel in range(4)}
    direct = take("r", 2)

    def farthest(s, right):
        return 4 if (s == 0) == right else 3

    two = {
        (layer, kind, s, right, d): take("r")
        for layer in range(LAYERS) for kind in range(2) for s in range(2) for right in (False, True)
        for d in range(1, 4)
    }
    two_end = take("r", LAYERS)

    next_to = [
        {k: dev(x, y, wrap(z + k, 8), c) for k in (1, -1)},
        {k: dev(x, wrap(y + k, 8), z, c) for k in (1, -1)},
    ]
    outer = [dev(x, y, wrap(z + out_z, 8), c), dev(x, wrap(y + out_y, 8), z, c)]
    mate = [dev(x, y, z - out_z, c), dev(x, y - out_y, z, c)]
    z_at = {k: wrap(z + k, 8) for k in range(-4, 5)}
    y_at = {k: (lax.div(wrap(y + k, 8), 2), lax.rem(wrap(y + k, 8), 2)) for k in range(-4, 5)}
    z_pair = lax.div(z, 2)
    pairs = [
        [z_pair * 2] + [wrap(z_pair + k, 4) * 2 for k in (out_z, -out_z, 2)],
        [yh] + [wrap(yh + k, 4) for k in (out_y, -out_y, 2)],
    ]

    def block(layer, kind, at_mate):
        if kind == 0:
            return w.at[layer, yh, z - out_z if at_mate else z, yl, 0]
        return w.at[layer, yh, z, 1 - yl if at_mate else yl, 1]

    def pair(layer, kind, rel, shift):
        if kind == 0:
            at = y_at[shift]
            return w.at[layer, at[0], pl.ds(pairs[0][rel], 2), at[1], 0]
        return w.at[layer, pairs[1][rel], z_at[shift], :, 1]

    def part(layer, kind, s, shift):
        if kind == 0:
            return w.at[layer, y_at[shift][0], pl.ds(4 * s, 4), y_at[shift][1], 0]
        return w.at[layer, pl.ds(2 * s, 2), z_at[shift], :, 1]

    batch_one = [[batch(w.at[layer, 0, pl.ds(0, 7), 0, 0]) for _ in range(2)] for layer in range(LAYERS)]
    batch_two = {
        (layer, kind, s): batch(w.at[layer, :, pl.ds(0, 6 if layer + kind + s == 0 else 7), 0, 0])
        for layer in range(LAYERS) for kind in range(2) for s in range(2)
    }
    lead = take("s")

    def pass_on(layer, kind, s, right, d):
        if d < farthest(s, right):
            piece = part(layer, kind, s, 0 if d == 0 else (-d if right else d))
            index = lead if right and layer + kind + s + d == 0 else batch_two[layer, kind, s]
            recv = two[layer, kind, s, right, d + 1] if d < 3 else two_end + layer
            send(piece, piece, recv, next_to[1 - kind][1 if right else -1], None, index)

    def ring(layer, s, d):
        for kind in range(2):
            for right in (False, True):
                if 1 <= d <= 3:
                    arrive(part(layer, kind, s, -d if right else d), two[layer, kind, s, right, d])
                pass_on(layer, kind, s, right, d)

    def ring_end(layer):
        arrive(w.at[layer, 0, :, :, 0], two_end + layer)

    def direct_send():
        for k in (1, -1, 2, -2, 3, -3, 4):
            for kind in range(2):
                mine = block(0, kind, False)
                to = wrap((z if kind == 0 else y) + k, 8)
                target = dev(x, y, to, c) if kind == 0 else dev(x, to, z, c)
                send(mine, mine, direct + kind, target, None, batch_one[0][kind])

    def direct_wait():
        for kind in range(2):
            arrive(w.at[0, 0, pl.ds(0, 7), 0, kind], direct + kind)

    def relay(t):
        for kind in range(2):
            if t == 0:
                mine = block(1, kind, False)
                send(mine, mine, one[kind, 0], mate[kind], None, batch_one[1][kind])
                continue
            rel = t - 1
            if rel == 0:
                arrive(block(1, kind, True), one[kind, 0])
            else:
                arrive(pair(1, kind, rel, 0), one[kind, rel])
            if rel < 3:
                piece = pair(1, kind, rel, 0)
                send(piece, piece, one[kind, rel + 1], (mate if rel == 1 else outer)[kind], None, batch_one[1][kind])

    spread_weights_wait(0)
    direct_send()
    spread_weights_wait(1)
    relay(0)
    direct_wait()
    ring(0, 0, 0)
    x0_all(x0_ring_send, False)
    relay(1)
    head = part(0, 0, 0, 0)
    pltpu.make_async_remote_copy(
        src_ref=head, dst_ref=head, send_sem=ssem.at[lead], recv_sem=rsem.at[0],
        device_id=partner, device_id_type=MESH,
    ).wait_send()
    ring(0, 1, 0)
    ring(0, 0, 1)
    relay(2)
    x0_all(x0_swap)
    last_send(0)
    ring(0, 1, 1)
    relay(3)
    ring(0, 0, 2)
    relay(4)
    ring(0, 1, 2)
    last_spread(0)
    ring(0, 0, 3)
    ring(1, 0, 0)
    ring(0, 1, 3)
    ring(1, 1, 0)
    last_swap(0)
    spread_cotangent()
    ring_end(0)
    arrive(x0.at[pl.ds(0, GROUP_ROWS), pl.ds(0, 1024)], x0_c)
    last_wait(0)

    pos_q = lax.broadcasted_iota(jnp.int32, (ROWS, GROUP_ROWS), 0)
    pos_k = lax.broadcasted_iota(jnp.int32, (ROWS, GROUP_ROWS), 1)

    def mask(j):
        s = 2 * group + j
        now = bound[s]
        prev = bound[jnp.maximum(s - 1, 0)]
        first = jnp.where(prev == ROWS, 0, prev)
        first = jnp.where(s > 0, first, ROWS)
        pos_m = pos_k - ROWS
        memory = (pos_k < ROWS) & (pos_q < now) & (pos_k >= first)
        segment = (pos_m >= 0) & (pos_m <= pos_q) & ((pos_m >= now) | (pos_q < now))
        return memory | segment

    halo_b = [take("r") for _ in range(LAYERS)]

    def project(layer, states, start=0, stop=3 * ROWS):
        def columns(row, first, last):
            total = None
            for part in range(4):
                weight = w[layer, part].reshape(512, 3 * BLK)[:, first:last]
                term = nn(states[row:stop, part * 512:(part + 1) * 512], weight)
                total = term if total is None else total + term
            return total.astype(BF)

        kv[layer, start:stop] = columns(start, BLK, 3 * BLK)
        own_start = max(start, ROWS)
        q[layer, own_start - ROWS:stop - ROWS] = columns(own_start, 0, BLK)

    def attend(layer, j):
        visible = mask(j)
        results = []
        for h in range(2):
            cols = slice(h * HEAD, (h + 1) * HEAD)
            vcols = slice(BLK + h * HEAD, BLK + (h + 1) * HEAD)
            queries = q[layer, j * ROWS:(j + 1) * ROWS, cols]
            keys = kv[layer, j * ROWS:(j + 2) * ROWS, cols]
            values = kv[layer, j * ROWS:(j + 2) * ROWS, vcols]
            scores = jnp.where(visible, nt(queries, keys) * SCALE, -1e30)
            raised = jnp.exp(scores - jnp.max(scores, axis=-1, keepdims=True))
            share = (raised / jnp.sum(raised, axis=-1, keepdims=True)).astype(BF)
            probs[layer, j, h] = share
            results.append(nn(share, values))
        return jnp.concatenate(results, axis=1)

    def x1_piece(j, xs, core):
        return quarter(1, (j + 1) * ROWS, xs, core)

    x1_x = [take("r", 3) for _ in range(2)]
    x1_c = take("r", 2)
    x1_sent = batch(x1.at[pl.ds(0, GROUP_ROWS), pl.ds(0, 1792)])

    def step_states(j):
        before_states = x0[(j + 1) * ROWS:(j + 2) * ROWS, pl.ds(own_col, BLK)]
        x1[(j + 1) * ROWS:(j + 2) * ROWS, pl.ds(own_col, BLK)] = (
            before_states.astype(F32) + attend(0, j)
        ).astype(BF)
        piece = x1_piece(j, x, c)
        for k in range(3):
            send(piece, piece, x1_x[j] + k, peers[k], None, x1_sent)
        send(piece, piece, x1_c + j, partner, None, x1_sent)

    def gather_states(j):
        for k in range(3):
            piece = x1_piece(j, wrap(x - k - 1, 4), c)
            arrive(piece, x1_x[j] + k)
            send(piece, piece, x1_c + j, partner, None, x1_sent)

    def gather_states_wait(j):
        arrive(x1.at[pl.ds((j + 1) * ROWS, ROWS), pl.ds(0, 1024)], x1_c + j)

    project(0, x0)
    ring(1, 0, 1)
    step_states(1)
    last_send(1)
    ring(1, 1, 1)
    step_states(0)
    ring(1, 0, 2)
    gather_states(1)
    ring(1, 1, 2)
    last_spread(1)
    gather_states(0)
    ring(1, 0, 3)
    ring(1, 1, 3)
    last_swap(1)
    gather_states_wait(1)
    gather_states_wait(0)
    ring_end(1)
    last_wait(1)
    project(1, x1, 0, 2 * ROWS)

    out_r = take("r", 2)

    def last_states(j):
        before_states = x1[(j + 1) * ROWS:(j + 2) * ROWS, pl.ds(own_col, BLK)]
        x2[j * ROWS:(j + 1) * ROWS, :] = (before_states.astype(F32) + attend(1, j)).astype(BF)
        dst = outbuf.at[:, pl.ds(pl.multiple_of(xl * BLK, BLK), BLK)]
        src = x2.at[pl.ds(j * ROWS, ROWS)]
        send(src, dst, out_r + xl, dev(2 * yl + j, dest_y, z, c), away[j])

        @pl.when(home[j])
        def _():
            outbuf[:, pl.ds(pl.multiple_of(xl * BLK, BLK), BLK)] = x2[j * ROWS:(j + 1) * ROWS, :]

    def backward_segment(layer, j, grad_out):
        dq, dk, dv = [], [], []
        for h in range(2):
            cols = slice(h * HEAD, (h + 1) * HEAD)
            vcols = slice(BLK + h * HEAD, BLK + (h + 1) * HEAD)
            queries = q[layer, j * ROWS:(j + 1) * ROWS, cols]
            keys = kv[layer, j * ROWS:(j + 2) * ROWS, cols]
            values = kv[layer, j * ROWS:(j + 2) * ROWS, vcols]
            share = probs[layer, j, h]
            g = grad_out[:, cols]
            dp = nt(g, values)
            wide = share.astype(F32)
            r = jnp.sum(wide * dp, axis=-1, keepdims=True)
            ds = (wide * (dp - r) * SCALE).astype(BF)
            dq.append(nn(ds, keys))
            dk.append(tn(ds, queries))
            dv.append(tn(share, g))
        dqkv[j * ROWS:(j + 1) * ROWS, :BLK] = jnp.concatenate(dq, axis=1).astype(BF)
        return jnp.concatenate(dk + dv, axis=1)

    swap_r = [take("r", 2) for _ in range(LAYERS)]
    swap_sent = [batch(swap_send.at[layer]) for layer in range(LAYERS)]

    def project_back(layer, j):
        rows = slice(j * ROWS, (j + 1) * ROWS)
        lhs = dqkv[rows, :]
        for i in range(2):
            weight = w[layer, 2 * i + other].reshape(512, 3 * BLK)
            swap_send[layer, rows, i * 512:(i + 1) * 512] = nt(lhs, weight).astype(BF)
        src = swap_send.at[layer, pl.ds(j * ROWS, ROWS)]
        send(src, swap_recv.at[layer, pl.ds(j * ROWS, ROWS)], swap_r[layer] + j, partner, None, swap_sent[layer])
        for i in range(2):
            weight = w[layer, 2 * i + c].reshape(512, 3 * BLK)
            own[rows, i * 512:(i + 1) * 512] = nt(lhs, weight)

    def back_first(layer, grad):
        both = backward_segment(layer, 0, grad)
        halo_send[layer] = both[:ROWS].astype(BF)
        send(halo_send.at[layer], halo_recv.at[layer], halo_b[layer], group_dev(before))
        dkv[:ROWS, :] = both[ROWS:]

    def back_second(layer, grad):
        both = backward_segment(layer, 1, grad)
        dkv[ROWS:, :] = both[:ROWS]
        dkv_last[...] = both[ROWS:]

    rs1_r = take("r", 2)
    rs1_sent = batch(rs_send.at[1, :, pl.ds(0, 768)])
    rs0_r = take("r", 4)
    mine = pl.multiple_of(x * BLK, BLK)

    def swapped(layer, j):
        rows = slice(j * ROWS, (j + 1) * ROWS)
        arrive(swap_recv.at[layer, pl.ds(j * ROWS, ROWS)], swap_r[layer] + j)
        return own[rows, :] + swap_recv[layer, rows, :].astype(F32)

    def sum_one(j):
        rows = slice(j * ROWS, (j + 1) * ROWS)
        total = swapped(1, j)
        own[rows, :] = total
        rs_send[1, rows, :] = total.astype(BF)
        for k in range(3):
            col = pl.multiple_of(wrap(x + k + 1, 4) * BLK, BLK)
            src = rs_send.at[1, pl.ds(j * ROWS, ROWS), pl.ds(col, BLK)]
            send(src, rs1_recv.at[k, pl.ds(j * ROWS, ROWS)], rs1_r + j, peers[k], None, rs1_sent)
        g1[rows, :] = cotg[rows, :].astype(F32) + own[rows, pl.ds(mine, BLK)]

    def summed_one(j):
        rows = slice(j * ROWS, (j + 1) * ROWS)
        arrive(rs1_recv.at[:, pl.ds(j * ROWS, ROWS)], rs1_r + j)
        g1[rows, :] = (
            g1[rows, :] + rs1_recv[0, rows, :].astype(F32)
            + rs1_recv[1, rows, :].astype(F32) + rs1_recv[2, rows, :].astype(F32)
        )

    def sum_last(j):
        rows = slice(j * ROWS, (j + 1) * ROWS)
        own[rows, pl.ds(mine, BLK)] = own[rows, pl.ds(mine, BLK)] + g1[rows, :]
        rs_send[0, rows, :] = swapped(0, j).astype(BF)
        for half in range(2):
            src = rs_send.at[0, pl.ds(j * ROWS, ROWS), pl.ds(half * 512, 512)]
            here = (x == 2 * yl + j) & (yl == half)
            send(src, rs0_recv.at[x], rs0_r + x, dev(2 * yl + j, yh * 2 + half, z, c), jnp.logical_not(here))

            @pl.when(here)
            def _():
                rs0_recv[x] = rs_send[0, rows, half * 512:(half + 1) * 512]

    def back_own(layer):
        dqkv[:ROWS, BLK:] = (dkv[:ROWS, :] + dkv[ROWS:, :]).astype(BF)
        project_back(layer, 0)

    def back_halo(layer):
        arrive(halo_recv.at[layer], halo_b[layer])
        dqkv[ROWS:, BLK:] = (dkv_last[...] + halo_recv[layer].astype(F32)).astype(BF)
        project_back(layer, 1)

    for k in range(2):
        arrive(cotg.at[pl.ds(k * ROWS, ROWS)], a2a_c + k, away[k])
    last_states(0)
    back_first(1, cotg[:ROWS, :])
    project(1, x1, 2 * ROWS, 3 * ROWS)
    last_states(1)
    back_second(1, cotg[ROWS:, :])
    back_own(1)
    sum_one(0)
    back_halo(1)
    sum_one(1)
    summed_one(0)
    back_first(0, g1[:ROWS, :].astype(BF))
    summed_one(1)
    back_second(0, g1[ROWS:, :].astype(BF))
    back_own(0)
    sum_last(0)
    back_halo(0)
    sum_last(1)

    for whole, index, cond in pending:
        copy = pltpu.make_async_remote_copy(
            src_ref=whole, dst_ref=whole, send_sem=ssem.at[index], recv_sem=rsem.at[0],
            device_id=partner, device_id_type=MESH,
        )
        when(cond, copy.wait_send)

    for k in range(2):
        arrive(outbuf.at[:, pl.ds(k * BLK, BLK)], out_r + k, away[k])
    out_ref[...] = outbuf[...]
    total = None
    for k in range(4):
        arrive(rs0_recv.at[k], rs0_r + k, jnp.logical_not(same & (x == k)))
    for k in range(4):
        term = rs0_recv[k].astype(F32)
        total = term if total is None else total + term
    grad_ref[...] = total

    assert counts["s"] <= N_SEND and counts["r"] <= N_RECV, counts


def per_device(inputs, cotangent, w_query, w_key, w_value, boundary):
    vmem = pl.BlockSpec(memory_space=pltpu.VMEM)
    scratch = [
        ((2, LAYERS, 16, 3 * BLK), BF),
        ((LAYERS, 4, 8, 2, 2, 16, 3 * BLK), BF),
        ((3 * ROWS, D), BF),
        ((3 * ROWS, D), BF),
        ((GROUP_ROWS, BLK), BF),
        ((LAYERS, 3 * ROWS, 2 * BLK), BF),
        ((LAYERS, GROUP_ROWS, BLK), BF),
        ((LAYERS, 2, 2, ROWS, GROUP_ROWS), BF),
        ((GROUP_ROWS, 2 * BLK), F32),
        ((ROWS, 2 * BLK), F32),
        ((LAYERS, ROWS, 2 * BLK), BF),
        ((LAYERS, ROWS, 2 * BLK), BF),
        ((GROUP_ROWS, 3 * BLK), BF),
        ((LAYERS, GROUP_ROWS, 1024), BF),
        ((LAYERS, GROUP_ROWS, 1024), BF),
        ((GROUP_ROWS, 1024), F32),
        ((LAYERS, GROUP_ROWS, 1024), BF),
        ((3, GROUP_ROWS, BLK), BF),
        ((4, ROWS, 512), BF),
        ((GROUP_ROWS, BLK), BF),
        ((ROWS, 512), BF),
        ((GROUP_ROWS, BLK), F32),
    ]
    return pl.pallas_call(
        kernel,
        out_shape=(
            jax.ShapeDtypeStruct((ROWS, 512), BF),
            jax.ShapeDtypeStruct((ROWS, 512), F32),
        ),
        in_specs=[pl.BlockSpec(memory_space=pl.ANY)] * 6,
        out_specs=(vmem, vmem),
        scratch_shapes=[pltpu.VMEM(shape, kind) for shape, kind in scratch]
        + [
            pltpu.VMEM((ROWS, 512), BF),
            pltpu.VMEM((ROWS, 512), BF),
            pltpu.SMEM((ROWS,), jnp.int32),
            pltpu.SemaphoreType.DMA((N_LOAD,)),
            pltpu.SemaphoreType.DMA((N_SEND,)), pltpu.SemaphoreType.DMA((N_RECV,)),
        ],
        compiler_params=pltpu.CompilerParams(
            collective_id=0, has_side_effects=True, vmem_limit_bytes=60 * 1024 * 1024
        ),
    )(inputs, cotangent, w_query, w_key, w_value, boundary)


def solution(mesh):
    return jax.shard_map(
        per_device,
        mesh=mesh,
        in_specs=(
            P("seg", "tp"),
            P("seg", "tp"),
            P(None, "seg", "tp"),
            P(None, "seg", "tp"),
            P(None, "seg", "tp"),
            P(),
        ),
        out_specs=(P("seg", "tp"), P("seg", "tp")),
        check_vma=False,
    )
```
